32 devices in a mesh: lon: 16 (over z, y, x), lat: 2 (over core).
Axes of the slice: x: 2, y: 2, z: 4, core: 2. Of those that a mesh axis runs over, the one named last changes fastest.
Arguments:
- potential_heat: float32 [4, 192, 2048], P(None, 'lat', 'lon'), may hold values from -6 to 6
- salt_anomaly_field: float32 [4, 192, 2048], P(None, 'lat', 'lon'), may hold values from -6 to 6
- zonal_current: float32 [4, 192, 2048], P(None, 'lat', 'lon'), may hold values from -6 to 6
- meridional_current: float32 [4, 192, 2048], P(None, 'lat', 'lon'), may hold values from -6 to 6
- water_indicator: int32 [4, 192, 2048], P(None, 'lat', 'lon'), may hold values 0 or 1
- floor_layer_index: int32 [192, 2048], P('lat', 'lon'), may hold values from 0 to 3
- zonal_spacing: float32 [192, 2048], P('lat', 'lon'), may hold values from 0.7 to 1.4
- meridional_spacing: float32 [192, 2048], P('lat', 'lon'), may hold values from 0.7 to 1.4
- planetary_rotation_factor: float32 [192, 2048], P('lat', 'lon'), may hold values from 0.3 to 1.5
- horizontal_eddy_coefficient: float32 [192, 2048], P('lat', 'lon'), may hold values from 0.05 to 0.25
- diapycnal_diffusivity: float32 [3, 192, 2048], P(None, 'lat', 'lon'), may hold values from 0.02 to 0.5
- layer_height: float32 [4], replicated, may hold values from 0.7 to 1.4
Outputs:
- new_temperature: float32 [4, 192, 2048], P(None, 'lat', 'lon')
- new_salinity: float32 [4, 192, 2048], P(None, 'lat', 'lon')
- new_zonal: float32 [4, 192, 2048], P(None, 'lat', 'lon')
- new_meridional: float32 [4, 192, 2048], P(None, 'lat', 'lon')
The draws below stay inside these ranges and needn't reach their ends.
All inputs are finite; a program needn't handle non-finite values. No bound on the sum of `water_indicator` on one device may be relied on, other than what follows from the above.
Results may differ from the reference program's by a relative error of at most 0.0003.
Values sent between devices are 32-bit elements; how exact they have to be, the bound alone decides.
A program may use at most 64 MiB of HBM per device.

```python
import math
import jax
import jax.numpy as jnp
from jax import lax

VERTICAL_LAYERS = 4
MERIDIAN_POINTS = 192
PARALLEL_POINTS = 2048


def set_ends(entries, own_key, least, largest):
    spot = [jax.random.randint(jax.random.fold_in(own_key, axis), (), 0, length) for axis, length in enumerate(entries.shape)]
    widest = entries.shape.index(max(entries.shape))
    neighbour = spot[:widest] + [(spot[widest] + 1) % entries.shape[widest]] + spot[widest + 1:]
    return entries.at[tuple(spot)].set(least).at[tuple(neighbour)].set(largest)


def level_of(own_key, extent, pieces, least, largest):
    gain, own = 1.0, jax.random.fold_in(own_key, 6)
    for axis_at, blocks in pieces:
        steps = jnp.exp(jax.random.uniform(jax.random.fold_in(own, axis_at), (blocks,), jnp.float32, least / len(pieces), largest / len(pieces)))
        gain = gain * jnp.repeat(steps, extent[axis_at] // blocks).reshape([-1 if axis == axis_at else 1 for axis in range(len(extent))])
    return gain


def bell_draw(own_key, extent, scale, bound, shards=(), held_as=jnp.bfloat16):
    values = scale * jax.random.normal(own_key, extent, jnp.float32)
    if shards:
        values = values * level_of(own_key, extent, shards, -0.22, 0.18)
    return jnp.clip(values, -bound, bound).astype(held_as)


def setup_inputs(seed: int = 0) -> dict:
    key_list = jax.random.split(jax.random.key(seed), 13)
    return {
        "potential_heat": bell_draw(key_list[0], (VERTICAL_LAYERS, MERIDIAN_POINTS, PARALLEL_POINTS), 1.0, 6.0, ((1, 2), (2, 16)), jnp.float32),
        "salt_anomaly_field": bell_draw(key_list[1], (VERTICAL_LAYERS, MERIDIAN_POINTS, PARALLEL_POINTS), 1.0, 6.0, ((1, 2), (2, 16)), jnp.float32),
        "zonal_current": bell_draw(key_list[2], (VERTICAL_LAYERS, MERIDIAN_POINTS, PARALLEL_POINTS), 1.0, 6.0, ((1, 2), (2, 16)), jnp.float32),
        "meridional_current": bell_draw(key_list[3], (VERTICAL_LAYERS, MERIDIAN_POINTS, PARALLEL_POINTS), 1.0, 6.0, ((1, 2), (2, 16)), jnp.float32),
        "water_indicator": set_ends((jax.random.randint(key_list[4], (VERTICAL_LAYERS, MERIDIAN_POINTS, PARALLEL_POINTS), 0, 10) < 9).astype(jnp.int32), jax.random.fold_in(key_list[4], 1), 0, 1),
        "floor_layer_index": set_ends(jax.random.randint(key_list[5], (MERIDIAN_POINTS, PARALLEL_POINTS), 0, VERTICAL_LAYERS), jax.random.fold_in(key_list[5], 1), 0, VERTICAL_LAYERS - 1).astype(jnp.int32),
        "zonal_spacing": jnp.clip(jnp.exp(math.log(1.4) - 0.6931472 * jax.random.uniform(key_list[6], (MERIDIAN_POINTS, PARALLEL_POINTS), jnp.float32) ** level_of(key_list[6], (MERIDIAN_POINTS, PARALLEL_POINTS), ((0, 2), (1, 16)), -0.2, 0.2)), 0.7, 1.4),
        "meridional_spacing": jnp.clip(jnp.exp(math.log(1.4) - 0.6931472 * jax.random.uniform(key_list[7], (MERIDIAN_POINTS, PARALLEL_POINTS), jnp.float32) ** level_of(key_list[7], (MERIDIAN_POINTS, PARALLEL_POINTS), ((0, 2), (1, 16)), -0.2, 0.2)), 0.7, 1.4),
        "planetary_rotation_factor": jnp.clip(jnp.exp(math.log(1.5) - 1.60943787 * jax.random.uniform(key_list[8], (MERIDIAN_POINTS, PARALLEL_POINTS), jnp.float32) ** level_of(key_list[8], (MERIDIAN_POINTS, PARALLEL_POINTS), ((0, 2), (1, 16)), -0.2, 0.2)), 0.3, 1.5),
        "horizontal_eddy_coefficient": jnp.clip(jnp.exp(math.log(0.25) - 1.609438 * jax.random.uniform(key_list[9], (MERIDIAN_POINTS, PARALLEL_POINTS), jnp.float32) ** level_of(key_list[9], (MERIDIAN_POINTS, PARALLEL_POINTS), ((0, 2), (1, 16)), -0.2, 0.2)), 0.05, 0.25),
        "diapycnal_diffusivity": jnp.clip(jnp.exp(math.log(0.5) - 3.218876 * jax.random.uniform(key_list[10], (VERTICAL_LAYERS - 1, MERIDIAN_POINTS, PARALLEL_POINTS), jnp.float32) ** level_of(key_list[10], (VERTICAL_LAYERS - 1, MERIDIAN_POINTS, PARALLEL_POINTS), ((1, 2), (2, 16)), -0.2, 0.2)), 0.02, 0.5),
        "layer_height": jnp.clip(jnp.exp(jax.random.uniform(key_list[11], (VERTICAL_LAYERS,), jnp.float32, math.log(0.7), math.log(1.4))), 0.7, 1.4),
    }


TIME_STEP = 0.25
EXPANSION = 0.2
CONTRACTION = 0.8
BOTTOM_DRAG = 1.0


def pressure(temp_part, salt_part, layer_height):
    layer_mass = (CONTRACTION * salt_part - EXPANSION * temp_part) * layer_height[:, None, None]
    return jnp.cumsum(layer_mass, axis=0) - 0.5 * layer_mass


def mix_vertically(fields, water_share, diapycnal_diffusivity, layer_height):
    contrast = fields[:, 1:] - fields[:, :-1]
    fluxes = diapycnal_diffusivity * (water_share[1:] * water_share[:-1]) * contrast
    boundary = jnp.zeros_like(fluxes[:, :1])
    flux_below = jnp.concatenate([fluxes, boundary], axis=1)
    flux_above = jnp.concatenate([boundary, fluxes], axis=1)
    return (flux_below - flux_above) / (layer_height * layer_height)[None, :, None, None]


def advance(central, eastern, western, northern, southern, floor_layer_index, zonal_spacing, meridional_spacing, planetary_rotation_factor, horizontal_eddy_coefficient, diapycnal_diffusivity, layer_height):
    levels = central.shape[1]
    at_bottom = (lax.broadcasted_iota(jnp.int32, (levels, 1, 1), 0) == floor_layer_index[None]).astype(jnp.float32)
    water_share = central[4]
    fields = central[:4]
    weight_east = water_share * eastern[4]
    weight_west = water_share * western[4]
    weight_north = water_share * northern[4]
    weight_south = water_share * southern[4]
    diffusion = horizontal_eddy_coefficient * ((weight_east * (eastern[:4] - fields) + weight_west * (western[:4] - fields)) / (zonal_spacing * zonal_spacing) + (weight_north * (northern[:4] - fields) + weight_south * (southern[:4] - fields)) / (meridional_spacing * meridional_spacing))
    zonal = fields[2]
    merid = fields[3]
    advection = -(zonal * (eastern[:4] - western[:4]) * (0.5 / zonal_spacing) + merid * (northern[:4] - southern[:4]) * (0.5 / meridional_spacing))
    pressure_east = pressure(eastern[0], eastern[1], layer_height)
    pressure_west = pressure(western[0], western[1], layer_height)
    pressure_north = pressure(northern[0], northern[1], layer_height)
    pressure_south = pressure(southern[0], southern[1], layer_height)
    gradient_x = -(pressure_east - pressure_west) * (0.5 / zonal_spacing)
    gradient_y = -(pressure_north - pressure_south) * (0.5 / meridional_spacing)
    mixing = mix_vertically(fields, water_share, diapycnal_diffusivity, layer_height)
    tendency = advection + diffusion + mixing
    tend_zonal = tendency[2] + planetary_rotation_factor * merid + gradient_x - BOTTOM_DRAG * at_bottom * zonal
    tend_merid = tendency[3] - planetary_rotation_factor * zonal + gradient_y - BOTTOM_DRAG * at_bottom * merid
    tendency = jnp.stack([tendency[0], tendency[1], tend_zonal, tend_merid])
    updated = water_share * (fields + TIME_STEP * tendency)
    return jnp.concatenate([updated, water_share[None]], axis=0)


def reference(potential_heat, salt_anomaly_field, zonal_current, meridional_current, water_indicator, floor_layer_index, zonal_spacing, meridional_spacing, planetary_rotation_factor, horizontal_eddy_coefficient, diapycnal_diffusivity, layer_height):
    water_share = water_indicator.astype(jnp.float32)
    combined_tracers = jnp.stack([potential_heat * water_share, salt_anomaly_field * water_share, zonal_current * water_share, meridional_current * water_share, water_share])
    fold_sign = jnp.array([1.0, 1.0, -1.0, -1.0, 1.0], jnp.float32).reshape(5, 1, 1, 1)
    channels, levels, lat_count, lon_count = combined_tracers.shape
    block_count = lat_count // 8
    for step_index in range(2):
        ghost_row = combined_tracers[:, :, -1:, ::-1] * fold_sign
        padded = jnp.concatenate([jnp.zeros_like(ghost_row), combined_tracers, ghost_row], axis=2)
        padded = jnp.concatenate([padded[..., -1:], padded, padded[..., :1]], axis=3)

        def one_block(block_index):
            row_start = (block_index * 8).astype(jnp.int32)
            window = lax.dynamic_slice_in_dim(padded, row_start, 10, 2)
            central = window[:, :, 1:-1, 1:-1]
            eastern = window[:, :, 1:-1, 2:]
            western = window[:, :, 1:-1, :-2]
            northern = window[:, :, 2:, 1:-1]
            southern = window[:, :, :-2, 1:-1]
            return advance(central, eastern, western, northern, southern,
                           lax.dynamic_slice_in_dim(floor_layer_index, row_start, 8, 0),
                           lax.dynamic_slice_in_dim(zonal_spacing, row_start, 8, 0),
                           lax.dynamic_slice_in_dim(meridional_spacing, row_start, 8, 0),
                           lax.dynamic_slice_in_dim(planetary_rotation_factor, row_start, 8, 0),
                           lax.dynamic_slice_in_dim(horizontal_eddy_coefficient, row_start, 8, 0),
                           lax.dynamic_slice_in_dim(diapycnal_diffusivity, row_start, 8, 1),
                           layer_height)

        results = lax.map(one_block, jnp.arange(block_count, dtype=jnp.int32))
        combined_tracers = jnp.moveaxis(results, 0, 2).reshape(channels, levels, lat_count, lon_count)
    return combined_tracers[0], combined_tracers[1], combined_tracers[2], combined_tracers[3]
```

```python
import functools

import jax
import jax.numpy as jnp
from jax import lax
from jax.experimental import pallas as pl
from jax.experimental.pallas import tpu as pltpu
from jax.sharding import PartitionSpec as P

MESH = pl.DeviceIdType.MESH
TIME_STEP = 0.25
EXPANSION = 0.2
CONTRACTION = 0.8
BOTTOM_DRAG = 1.0
LEVELS = 4
ENTRIES = 28
WET = 4
PAD = 8


def coefficients(w, we, ww, wn, ws, metrics, inv_h2):
    floor, zs, ms, rot, eddy = metrics[:5]
    mix = metrics[5:]
    rz, rm = 1.0 / zs, 1.0 / ms
    kx, ky = eddy * rz * rz, eddy * rm * rm
    hx, hy = 0.5 * rz, 0.5 * rm
    out = []
    for k in range(LEVELS):
        dtw = TIME_STEP * w[k]
        ax, ay = dtw * kx, dtw * ky
        ae, aw, an, as_ = ax * we[k], ax * ww[k], ay * wn[k], ay * ws[k]
        centre = 1.0 - (ae + aw) - (an + as_)
        t = dtw * inv_h2[k]
        below = above = None
        if k < LEVELS - 1:
            below = t * mix[k] * w[k + 1]
            centre = centre - below
        if k > 0:
            above = t * mix[k - 1] * w[k - 1]
            centre = centre - above
        drag = centre - jnp.where(floor == float(k), BOTTOM_DRAG * dtw, 0.0)
        out.append((ae, aw, an, as_, centre, drag, dtw * hx, dtw * hy, dtw * rot, below, above))
    return out


def advance(f, east, west, north, south, coef, heights):
    new = [[None] * LEVELS for _ in range(4)]
    sum_x = sum_y = None
    for k in range(LEVELS):
        ae, aw, an, as_, centre, drag, bx, by, rot, below, above = coef[k]
        u, v = f[2][k], f[3][k]
        bu, bv = bx * u, by * v
        ce, cw, cn, cs = ae - bu, aw + bu, an - bv, as_ + bv
        layer_x = (CONTRACTION * (east[1][k] - west[1][k]) - EXPANSION * (east[0][k] - west[0][k])) * heights[k]
        layer_y = (CONTRACTION * (north[1][k] - south[1][k]) - EXPANSION * (north[0][k] - south[0][k])) * heights[k]
        sum_x = layer_x if sum_x is None else sum_x + layer_x
        sum_y = layer_y if sum_y is None else sum_y + layer_y
        for c in range(4):
            val = ((centre if c < 2 else drag) * f[c][k] + (ce * east[c][k] + cw * west[c][k])
                   + (cn * north[c][k] + cs * south[c][k]))
            if below is not None:
                val = val + below * f[c][k + 1]
            if above is not None:
                val = val + above * f[c][k - 1]
            if c == 2:
                val = val + rot * v - bx * (sum_x - 0.5 * layer_x)
            if c == 3:
                val = val - rot * u - by * (sum_y - 0.5 * layer_y)
            new[c][k] = val
    return new


def kernel(nlon, nlat, rows, cols, *refs):
    ins, h_ref = refs[:11], refs[11]
    outs = refs[12:16]
    (x4, wet_i, floor_i, met, mix, x, y, coef_s, pack, ext, send_r, recv_r, corner, slab_c, slab_r, z,
     in_sem, out_sem, s_sem, r_sem) = refs[16:]
    lon, lat = lax.axis_index("lon"), lax.axis_index("lat")
    top, bottom = lat == nlat - 1, lat == 0
    f32 = jnp.float32

    loads = [pltpu.make_async_copy(ins[c], x4.at[c], in_sem.at[c]) for c in range(4)]
    loads.append(pltpu.make_async_copy(ins[4], wet_i, in_sem.at[4]))
    loads.append(pltpu.make_async_copy(ins[5], floor_i, in_sem.at[5]))
    loads += [pltpu.make_async_copy(ins[6 + m], met.at[m], in_sem.at[6 + m]) for m in range(4)]
    loads.append(pltpu.make_async_copy(ins[10], mix, in_sem.at[10]))
    for load in loads:
        load.start()

    e_lon, w_lon = lax.rem(lon + 1, nlon), lax.rem(lon + nlon - 1, nlon)
    n_lat = jnp.where(top, lat, lat + 1)
    n_lon = jnp.where(top, nlon - 1 - lon, lon)
    ne_lon = jnp.where(top, lax.rem(2 * nlon - 2 - lon, nlon), e_lon)
    nw_lon = jnp.where(top, lax.rem(nlon - lon, nlon), w_lon)
    s_lat = jnp.maximum(lat - 1, 0)
    ne_self = jnp.logical_and(top, ne_lon == lon)
    nw_self = jnp.logical_and(top, nw_lon == lon)
    ne_other = jnp.logical_not(ne_self)
    nw_other = jnp.logical_not(nw_self)
    inner = jnp.logical_not(bottom)

    for side in range(2):
        ext[side, rows:, :] = jnp.zeros((128 - rows, 128), f32)

    @pl.when(bottom)
    def _():
        recv_r[1, : 2 * 5 * LEVELS, :] = jnp.zeros((2 * 5 * LEVELS, cols), f32)
        recv_r[1, 2 * 5 * LEVELS :, :] = jnp.ones((2 * ENTRIES - 10 * LEVELS, cols), f32)

    barrier = pltpu.get_barrier_semaphore()

    def greet(dev):
        pl.semaphore_signal(barrier, inc=1, device_id=dev, device_id_type=MESH)

    greet((e_lon, lat))
    greet((w_lon, lat))
    greet((n_lon, n_lat))

    @pl.when(ne_other)
    def _():
        greet((ne_lon, n_lat))

    @pl.when(nw_other)
    def _():
        greet((nw_lon, n_lat))

    @pl.when(inner)
    def _():
        greet((lon, s_lat))
        greet((e_lon, s_lat))
        greet((w_lon, s_lat))

    lane = lax.broadcasted_iota(jnp.int32, (8, 128), 1)
    sub = lax.broadcasted_iota(jnp.int32, (8, 128), 0)
    heights = [jnp.full((8, 128), h_ref[k], f32) for k in range(LEVELS)]
    inv_h2 = [1.0 / (h * h) for h in heights]

    for load in loads:
        load.wait()

    chunks = rows // 8
    mets = [None, met.at[0], met.at[1], met.at[2], met.at[3], mix.at[0], mix.at[1], mix.at[2]]

    def metric(m, span):
        return floor_i[span, :].astype(f32) if m == 0 else mets[m][span, :]

    for r in range(chunks):
        span = pl.ds(8 * r, 8)
        held = pl.ds(PAD + 8 * r, 8)
        packed = jnp.zeros((8, 128), f32)
        wet = [wet_i[k, span, :].astype(f32) for k in range(LEVELS)]
        for c in range(ENTRIES):
            ch, k = c // LEVELS, c % LEVELS
            if ch < 4:
                val = x4[ch, k, span, :] * wet[k]
            elif ch == WET:
                val = wet[k]
            else:
                val = metric(c - 5 * LEVELS, span)
            if ch <= WET:
                x[ch, k, held, :] = val
            packed = jnp.where(lane // 4 == c, pltpu.roll(val, (4 * c + 2) % 128, 1), packed)
        pack[span, :] = packed

    def own_rows(c, first):
        ch, k = c // LEVELS, c % LEVELS
        if ch <= WET:
            return x[ch, k, pl.ds(PAD + first, 2), :]
        return metric(c - 5 * LEVELS, pl.ds(first, 2))

    for c in range(ENTRIES):
        low, high = own_rows(c, 0), own_rows(c, rows - 2)
        send_r[1, pl.ds(2 * c, 2), :] = low
        send_r[0, pl.ds(2 * c, 2), :] = high
        slab_r[c, 0:2, :] = high
        slab_r[c, 6:8, :] = low

    @pl.when(top)
    def _():
        for t in range(2 * ENTRIES // 8):
            val = send_r[0, pl.ds(8 * t, 8), :]
            val = jnp.where(sub % 2 == 1, pltpu.roll(val, 1, 0), pltpu.roll(val, 7, 0))
            step = 1
            while step < cols:
                val = jnp.where((lane // step) % 2 == 1, pltpu.roll(val, step, 1), pltpu.roll(val, cols - step, 1))
                step *= 2
            if 16 * LEVELS // 4 <= 8 * t < 32 * LEVELS // 4:
                val = -val
            send_r[0, pl.ds(8 * t, 8), :] = val

    last = pack[pl.ds(rows - 8, 8), :]
    turned = jnp.broadcast_to(last[7:8, :], (8, 128))
    for step in (1, 2):
        turned = jnp.where((lane // step) % 2 == 1, pltpu.roll(turned, step, 1), pltpu.roll(turned, 128 - step, 1))
    turned = jnp.where(jnp.logical_and(lane >= 8 * LEVELS, lane < 16 * LEVELS), -turned, turned)
    top_v = jnp.full((8, 128), top.astype(jnp.int32)) == 1
    folded = jnp.where(top_v, turned, last)
    corner[...] = folded

    @pl.when(ne_self)
    def _():
        ext[0, pl.ds(rows, 8), :] = folded

    @pl.when(nw_self)
    def _():
        ext[1, pl.ds(rows, 8), :] = folded

    pl.semaphore_wait(
        barrier,
        3 + ne_other.astype(jnp.int32) + nw_other.astype(jnp.int32) + 3 * inner.astype(jnp.int32),
    )

    def copy(src, dst, s, r, dev):
        return pltpu.make_async_remote_copy(
            src_ref=src, dst_ref=dst, send_sem=s_sem.at[s], recv_sem=r_sem.at[r], device_id=dev, device_id_type=MESH
        )

    body, up, down = pl.ds(0, rows), pl.ds(rows, 8), pl.ds(120, 8)
    to_east = copy(pack, ext.at[1, body], 0, 1, (e_lon, lat))
    to_west = copy(pack, ext.at[0, body], 1, 0, (w_lon, lat))
    fold_n = copy(send_r.at[0], recv_r.at[0], 2, 2, (n_lon, n_lat))
    fold_ne = copy(corner, ext.at[0, up], 4, 4, (ne_lon, n_lat))
    fold_nw = copy(corner, ext.at[1, up], 5, 5, (nw_lon, n_lat))
    to_n = copy(send_r.at[0], recv_r.at[1], 2, 3, (n_lon, n_lat))
    to_ne = copy(corner, ext.at[1, down], 4, 7, (ne_lon, n_lat))
    to_nw = copy(corner, ext.at[0, down], 5, 6, (nw_lon, n_lat))
    to_s = copy(send_r.at[1], recv_r.at[0], 3, 2, (lon, s_lat))
    to_se = copy(pack.at[pl.ds(0, 8)], ext.at[1, up], 6, 5, (e_lon, s_lat))
    to_sw = copy(pack.at[pl.ds(0, 8)], ext.at[0, up], 7, 4, (w_lon, s_lat))

    @pl.when(top)
    def _():
        fold_n.start()

    to_east.start()
    to_west.start()

    @pl.when(jnp.logical_and(top, ne_other))
    def _():
        fold_ne.start()

    @pl.when(jnp.logical_and(top, nw_other))
    def _():
        fold_nw.start()

    @pl.when(jnp.logical_not(top))
    def _():
        to_n.start()
        to_ne.start()
        to_nw.start()

    @pl.when(inner)
    def _():
        to_s.start()
        to_se.start()
        to_sw.start()

    to_s.wait_recv()

    @pl.when(inner)
    def _():
        to_n.wait_recv()
        to_ne.wait_recv()
        to_nw.wait_recv()

    @pl.when(ne_other)
    def _():
        to_sw.wait_recv()

    @pl.when(nw_other)
    def _():
        to_se.wait_recv()

    to_west.wait_recv()
    to_east.wait_recv()

    first_half = lane % 4 < 2
    for c in range(5 * LEVELS):
        ch, k = c // LEVELS, c % LEVELS
        x[ch, k, pl.ds(PAD + rows, 1), :] = recv_r[0, pl.ds(2 * c, 1), :]
        x[ch, k, pl.ds(PAD - 1, 1), :] = recv_r[1, pl.ds(2 * c + 1, 1), :]
    for c in range(ENTRIES):
        slab_r[c, 2:4, :] = recv_r[0, pl.ds(2 * c, 2), :]
        slab_r[c, 4:6, :] = recv_r[1, pl.ds(2 * c, 2), :]

    def side_of(hold, c, val):
        ends = pltpu.roll(hold, (128 - (4 * c + 2)) % 128, 1)
        east = pltpu.roll(jnp.where(lane == 0, ends, val), 127, 1)
        west = pltpu.roll(jnp.where(lane == 127, ends, val), 1, 1)
        return east, west

    def grid_of(fn):
        return [[fn(ch, k) for k in range(LEVELS)] for ch in range(5)]

    filler = jnp.zeros((128 - rows, 128), f32)
    own = jnp.concatenate([pack[...], filler], axis=0)
    half = lax.broadcasted_iota(jnp.int32, (128, 128), 1) % 4 < 2
    east_t = jnp.transpose(jnp.where(half, own, ext[0]))
    west_t = jnp.transpose(jnp.where(half, ext[1], own))
    for c in range(ENTRIES):
        slab_c[c, 0:4, :] = east_t[4 * c : 4 * c + 4, :]
        slab_c[c, 4:8, :] = west_t[4 * c : 4 * c + 4, :]

    def slab_step(slab, shifts):
        f = grid_of(lambda ch, k: slab[ch * LEVELS + k])
        e, w, n, s = shifts(f)
        metrics = [slab[5 * LEVELS + m] for m in range(8)]
        cf = coefficients(f[WET], e[WET], w[WET], n[WET], s[WET], metrics, inv_h2)
        return advance(f, e, w, n, s, cf, heights)

    def each(f, fn):
        return [[fn(ch, k, f[ch][k]) for k in range(LEVELS)] for ch in range(5)]

    def shifts_c(f):
        return (
            each(f, lambda ch, k, a: pltpu.roll(a, 7, 0)),
            each(f, lambda ch, k, a: pltpu.roll(a, 1, 0)),
            each(f, lambda ch, k, a: pltpu.roll(a, 127, 1)),
            each(f, lambda ch, k, a: pltpu.roll(a, 1, 1)),
        )

    z[...] = jnp.zeros((128, 128), f32)
    new = slab_step(slab_c, shifts_c)
    for c in range(4 * LEVELS):
        val = new[c // LEVELS][c % LEVELS]
        z[pl.ds(4 * c + 1, 1), :] = val[5:6, :]
        z[pl.ds(4 * c + 2, 1), :] = val[2:3, :]
    z[...] = jnp.transpose(z[...])

    is_east = lane % 4 == 2
    far_n = jnp.where(is_east, ext[0, up, :], ext[1, up, :])[0:1, :]
    far_s = jnp.where(is_east, ext[0, down, :], ext[1, down, :])[7:8, :]
    far = jnp.where(sub == 2, jnp.broadcast_to(far_n, (8, 128)), jnp.broadcast_to(far_s, (8, 128)))

    def shifts_r(f):
        pairs = each(f, lambda ch, k, a: side_of(far, ch * LEVELS + k, a))
        return (
            [[p[0] for p in line] for line in pairs],
            [[p[1] for p in line] for line in pairs],
            each(f, lambda ch, k, a: pltpu.roll(a, 7, 0)),
            each(f, lambda ch, k, a: pltpu.roll(a, 1, 0)),
        )

    new = slab_step(slab_r, shifts_r)
    for c in range(4 * LEVELS):
        val = new[c // LEVELS][c % LEVELS]
        y[c // LEVELS, c % LEVELS, pl.ds(PAD + rows, 1), :] = val[2:3, :]
        y[c // LEVELS, c % LEVELS, pl.ds(PAD - 1, 1), :] = val[5:6, :]

    def main_step(src, r, hold, channels):
        pick = lambda shift: [
            [src[ch, k, pl.ds(PAD + 8 * r + shift, 8), :] for k in range(LEVELS)] for ch in range(channels)
        ]
        f = pick(0)
        pairs = [[side_of(hold, ch * LEVELS + k, f[ch][k]) for k in range(LEVELS)] for ch in range(channels)]
        return (
            f,
            [[p[0] for p in line] for line in pairs],
            [[p[1] for p in line] for line in pairs],
            pick(1),
            pick(-1),
        )

    for r in range(chunks):
        span = pl.ds(8 * r, 8)
        hold = jnp.where(is_east, ext[0, span, :], ext[1, span, :])
        f, e, w, n, s = main_step(x, r, hold, 5)
        metrics = [metric(m, span) for m in range(8)]
        cf = coefficients(f[WET], e[WET], w[WET], n[WET], s[WET], metrics, inv_h2)
        new = advance(f, e, w, n, s, cf, heights)
        for k in range(LEVELS):
            for i, val in enumerate(cf[k]):
                if val is not None:
                    coef_s[i, k, span, :] = val
            for ch in range(4):
                y[ch, k, pl.ds(PAD + 8 * r, 8), :] = new[ch][k]

    for r in range(chunks):
        span = pl.ds(8 * r, 8)
        f, e, w, n, s = main_step(y, r, z[span, :], 4)
        cf = []
        for k in range(LEVELS):
            absent = {9} if k == LEVELS - 1 else ({10} if k == 0 else set())
            cf.append(tuple(None if i in absent else coef_s[i, k, span, :] for i in range(11)))
        new = advance(f, e, w, n, s, cf, heights)
        for ch in range(4):
            for k in range(LEVELS):
                x4[ch, k, span, :] = new[ch][k]

    stores = [pltpu.make_async_copy(x4.at[c], outs[c], out_sem.at[c]) for c in range(4)]
    for store in stores:
        store.start()

    to_east.wait_send()
    to_west.wait_send()
    to_n.wait_send()

    @pl.when(ne_other)
    def _():
        to_ne.wait_send()

    @pl.when(nw_other)
    def _():
        to_nw.wait_send()

    @pl.when(inner)
    def _():
        to_s.wait_send()
        to_se.wait_send()
        to_sw.wait_send()

    for store in stores:
        store.wait()


def solution(mesh):
    nlon, nlat = mesh.shape["lon"], mesh.shape["lat"]

    def shards(*args):
        levels, rows, cols = args[0].shape
        f32 = jnp.float32
        vmem = pltpu.VMEM
        return tuple(pl.pallas_call(
            functools.partial(kernel, nlon, nlat, rows, cols),
            out_shape=[jax.ShapeDtypeStruct((levels, rows, cols), f32)] * 4,
            in_specs=[pl.BlockSpec(memory_space=pl.ANY)] * 11 + [pl.BlockSpec(memory_space=pltpu.SMEM)],
            out_specs=[pl.BlockSpec(memory_space=pl.ANY)] * 4,
            scratch_shapes=[
                vmem((4, levels, rows, cols), f32),
                vmem((levels, rows, cols), jnp.int32),
                vmem((rows, cols), jnp.int32),
                vmem((4, rows, cols), f32),
                vmem((levels - 1, rows, cols), f32),
                vmem((5, levels, rows + 2 * PAD, cols), f32),
                vmem((4, levels, rows + 2 * PAD, cols), f32),
                vmem((11, levels, rows, cols), f32),
                vmem((rows, 128), f32),
                vmem((2, 128, 128), f32),
                vmem((2, 2 * ENTRIES, cols), f32),
                vmem((2, 2 * ENTRIES, cols), f32),
                vmem((8, 128), f32),
                vmem((ENTRIES, 8, 128), f32),
                vmem((ENTRIES, 8, cols), f32),
                vmem((128, 128), f32),
                pltpu.SemaphoreType.DMA((11,)),
                pltpu.SemaphoreType.DMA((4,)),
                pltpu.SemaphoreType.DMA((8,)),
                pltpu.SemaphoreType.DMA((8,)),
            ],
            compiler_params=pltpu.CompilerParams(
                collective_id=0, has_side_effects=True, vmem_limit_bytes=32 * 1024 * 1024
            ),
        )(*args))

    field, plane = P(None, "lat", "lon"), P("lat", "lon")
    return jax.shard_map(
        shards,
        mesh=mesh,
        in_specs=(field,) * 5 + (plane,) * 5 + (field, P()),
        out_specs=(field,) * 4,
        check_vma=False,
    )
```

```python
import functools

import jax
import jax.numpy as jnp
from jax import lax
from jax.experimental import pallas as pl
from jax.experimental.pallas import tpu as pltpu
from jax.sharding import PartitionSpec as P

MESH = pl.DeviceIdType.MESH
TIME_STEP = 0.25
EXPANSION = 0.2
CONTRACTION = 0.8
BOTTOM_DRAG = 1.0
LEVELS = 4
ENTRIES = 28
WET = 4
PAD = 8


def level_coefficients(k, w, we, ww, wn, ws, metrics, inv_h2, w_below, w_above):
    floor, zs, ms, rot, eddy = metrics[:5]
    mix = metrics[5:]
    rz, rm = 1.0 / zs, 1.0 / ms
    dtw = TIME_STEP * w
    ax, ay = dtw * (eddy * rz * rz), dtw * (eddy * rm * rm)
    ae, aw, an, as_ = ax * we, ax * ww, ay * wn, ay * ws
    centre = 1.0 - (ae + aw) - (an + as_)
    t = dtw * inv_h2[k]
    below = above = None
    if k < LEVELS - 1:
        below = t * mix[k] * w_below
        centre = centre - below
    if k > 0:
        above = t * mix[k - 1] * w_above
        centre = centre - above
    drag = centre - jnp.where(floor == float(k), BOTTOM_DRAG * dtw, 0.0)
    return ae, aw, an, as_, centre, drag, dtw * (0.5 * rz), dtw * (0.5 * rm), dtw * rot, below, above


def advance_level(k, f, f_below, f_above, east, west, north, south, coef, heights, sums):
    ae, aw, an, as_, centre, drag, bx, by, rot, below, above = coef
    u, v = f[2], f[3]
    bu, bv = bx * u, by * v
    ce, cw, cn, cs = ae - bu, aw + bu, an - bv, as_ + bv
    layer_x = (CONTRACTION * (east[1] - west[1]) - EXPANSION * (east[0] - west[0])) * heights[k]
    layer_y = (CONTRACTION * (north[1] - south[1]) - EXPANSION * (north[0] - south[0])) * heights[k]
    sum_x, sum_y = (layer_x, layer_y) if k == 0 else (sums[0] + layer_x, sums[1] + layer_y)
    new = []
    for c in range(4):
        val = ((centre if c < 2 else drag) * f[c] + (ce * east[c] + cw * west[c])
               + (cn * north[c] + cs * south[c]))
        if below is not None:
            val = val + below * f_below[c]
        if above is not None:
            val = val + above * f_above[c]
        if c == 2:
            val = val + rot * v - bx * (sum_x - 0.5 * layer_x)
        if c == 3:
            val = val - rot * u - by * (sum_y - 0.5 * layer_y)
        new.append(val)
    return new, (sum_x, sum_y)


def kernel(nlon, nlat, rows, cols, *refs):
    ins, h_ref = refs[:11], refs[11]
    outs = refs[12:16]
    (x4, wet_i, floor_i, met, mix, x, y, coef_s, pack, ext, send_r, recv_r, corner, slab_c, slab_r, z,
     in_sem, out_sem, s_sem, r_sem) = refs[16:]
    lon, lat = lax.axis_index("lon"), lax.axis_index("lat")
    top, bottom = lat == nlat - 1, lat == 0
    f32 = jnp.float32

    loads = [pltpu.make_async_copy(ins[c], x4.at[c], in_sem.at[c]) for c in range(4)]
    loads.append(pltpu.make_async_copy(ins[4], wet_i, in_sem.at[4]))
    loads.append(pltpu.make_async_copy(ins[5], floor_i, in_sem.at[5]))
    loads += [pltpu.make_async_copy(ins[6 + m], met.at[m], in_sem.at[6 + m]) for m in range(4)]
    loads.append(pltpu.make_async_copy(ins[10], mix, in_sem.at[10]))
    for load in loads:
        load.start()

    e_lon, w_lon = lax.rem(lon + 1, nlon), lax.rem(lon + nlon - 1, nlon)
    n_lat = jnp.where(top, lat, lat + 1)
    n_lon = jnp.where(top, nlon - 1 - lon, lon)
    ne_lon = jnp.where(top, lax.rem(2 * nlon - 2 - lon, nlon), e_lon)
    nw_lon = jnp.where(top, lax.rem(nlon - lon, nlon), w_lon)
    s_lat = jnp.maximum(lat - 1, 0)
    ne_self = jnp.logical_and(top, ne_lon == lon)
    nw_self = jnp.logical_and(top, nw_lon == lon)
    ne_other = jnp.logical_not(ne_self)
    nw_other = jnp.logical_not(nw_self)
    inner = jnp.logical_not(bottom)

    for side in range(2):
        ext[side, rows:, :] = jnp.zeros((128 - rows, 128), f32)

    @pl.when(bottom)
    def _():
        recv_r[1, : 2 * 5 * LEVELS, :] = jnp.zeros((2 * 5 * LEVELS, cols), f32)
        recv_r[1, 2 * 5 * LEVELS :, :] = jnp.ones((2 * ENTRIES - 10 * LEVELS, cols), f32)

    barrier = pltpu.get_barrier_semaphore()

    def greet(dev):
        pl.semaphore_signal(barrier, inc=1, device_id=dev, device_id_type=MESH)

    greet((e_lon, lat))
    greet((w_lon, lat))
    greet((n_lon, n_lat))

    @pl.when(ne_other)
    def _():
        greet((ne_lon, n_lat))

    @pl.when(nw_other)
    def _():
        greet((nw_lon, n_lat))

    @pl.when(inner)
    def _():
        greet((lon, s_lat))
        greet((e_lon, s_lat))
        greet((w_lon, s_lat))

    lane = lax.broadcasted_iota(jnp.int32, (8, 128), 1)
    sub = lax.broadcasted_iota(jnp.int32, (8, 128), 0)
    heights = [jnp.full((8, 128), h_ref[k], f32) for k in range(LEVELS)]
    inv_h2 = [1.0 / (h * h) for h in heights]

    for load in loads:
        load.wait()

    chunks = rows // 8
    mets = [None, met.at[0], met.at[1], met.at[2], met.at[3], mix.at[0], mix.at[1], mix.at[2]]

    def metric(m, span):
        return floor_i[span, :].astype(f32) if m == 0 else mets[m][span, :]

    group = lane >> 2

    @pl.loop(0, chunks)
    def _(r):
        span = pl.ds(pl.multiple_of(8 * r, 8), 8)
        held = pl.ds(pl.multiple_of(PAD + 8 * r, 8), 8)
        packed = jnp.zeros((8, 128), f32)
        wet = [wet_i[k, span, :].astype(f32) for k in range(LEVELS)]
        for c in range(ENTRIES):
            ch, k = c // LEVELS, c % LEVELS
            if ch < 4:
                val = x4[ch, k, span, :] * wet[k]
            elif ch == WET:
                val = wet[k]
            else:
                val = metric(c - 5 * LEVELS, span)
            if ch <= WET:
                x[ch, k, held, :] = val
            packed = jnp.where(group == c, pltpu.roll(val, (4 * c + 2) % 128, 1), packed)
        pack[span, :] = packed

    def own_rows(c, first):
        ch, k = c // LEVELS, c % LEVELS
        if ch <= WET:
            return x[ch, k, pl.ds(PAD + first, 2), :]
        return metric(c - 5 * LEVELS, pl.ds(first, 2))

    for c in range(ENTRIES):
        low, high = own_rows(c, 0), own_rows(c, rows - 2)
        send_r[1, pl.ds(2 * c, 2), :] = low
        send_r[0, pl.ds(2 * c, 2), :] = high
        slab_r[c, 0:2, :] = high
        slab_r[c, 6:8, :] = low

    @pl.when(top)
    def _():
        @pl.loop(0, 2 * ENTRIES // 8)
        def _(t):
            span = pl.ds(pl.multiple_of(8 * t, 8), 8)
            val = send_r[0, span, :]
            val = jnp.where((sub & 1) == 1, pltpu.roll(val, 1, 0), pltpu.roll(val, 7, 0))
            step = 1
            while step < cols:
                val = jnp.where((lane & step) != 0, pltpu.roll(val, step, 1), pltpu.roll(val, cols - step, 1))
                step *= 2
            flipped = jnp.logical_and(8 * t + sub >= 4 * LEVELS, 8 * t + sub < 8 * LEVELS)
            send_r[0, span, :] = jnp.where(flipped, -val, val)

    last = pack[pl.ds(rows - 8, 8), :]
    turned = jnp.broadcast_to(last[7:8, :], (8, 128))
    for step in (1, 2):
        turned = jnp.where((lane & step) != 0, pltpu.roll(turned, step, 1), pltpu.roll(turned, 128 - step, 1))
    turned = jnp.where(jnp.logical_and(lane >= 8 * LEVELS, lane < 16 * LEVELS), -turned, turned)
    top_v = jnp.full((8, 128), top.astype(jnp.int32)) == 1
    folded = jnp.where(top_v, turned, last)
    corner[...] = folded

    @pl.when(ne_self)
    def _():
        ext[0, pl.ds(rows, 8), :] = folded

    @pl.when(nw_self)
    def _():
        ext[1, pl.ds(rows, 8), :] = folded

    pl.semaphore_wait(
        barrier,
        3 + ne_other.astype(jnp.int32) + nw_other.astype(jnp.int32) + 3 * inner.astype(jnp.int32),
    )

    def copy(src, dst, s, r, dev):
        return pltpu.make_async_remote_copy(
            src_ref=src, dst_ref=dst, send_sem=s_sem.at[s], recv_sem=r_sem.at[r], device_id=dev, device_id_type=MESH
        )

    body, up, down = pl.ds(0, rows), pl.ds(rows, 8), pl.ds(120, 8)
    to_east = copy(pack, ext.at[1, body], 0, 1, (e_lon, lat))
    to_west = copy(pack, ext.at[0, body], 1, 0, (w_lon, lat))
    fold_n = copy(send_r.at[0], recv_r.at[0], 2, 2, (n_lon, n_lat))
    fold_ne = copy(corner, ext.at[0, up], 4, 4, (ne_lon, n_lat))
    fold_nw = copy(corner, ext.at[1, up], 5, 5, (nw_lon, n_lat))
    to_n = copy(send_r.at[0], recv_r.at[1], 2, 3, (n_lon, n_lat))
    to_ne = copy(corner, ext.at[1, down], 4, 7, (ne_lon, n_lat))
    to_nw = copy(corner, ext.at[0, down], 5, 6, (nw_lon, n_lat))
    to_s = copy(send_r.at[1], recv_r.at[0], 3, 2, (lon, s_lat))
    to_se = copy(pack.at[pl.ds(0, 8)], ext.at[1, up], 6, 5, (e_lon, s_lat))
    to_sw = copy(pack.at[pl.ds(0, 8)], ext.at[0, up], 7, 4, (w_lon, s_lat))

    @pl.when(top)
    def _():
        fold_n.start()

    to_east.start()
    to_west.start()

    @pl.when(jnp.logical_and(top, ne_other))
    def _():
        fold_ne.start()

    @pl.when(jnp.logical_and(top, nw_other))
    def _():
        fold_nw.start()

    @pl.when(jnp.logical_not(top))
    def _():
        to_n.start()
        to_ne.start()
        to_nw.start()

    @pl.when(inner)
    def _():
        to_s.start()
        to_se.start()
        to_sw.start()

    to_s.wait_recv()

    @pl.when(inner)
    def _():
        to_n.wait_recv()
        to_ne.wait_recv()
        to_nw.wait_recv()

    @pl.when(ne_other)
    def _():
        to_sw.wait_recv()

    @pl.when(nw_other)
    def _():
        to_se.wait_recv()

    to_west.wait_recv()
    to_east.wait_recv()

    for c in range(5 * LEVELS):
        ch, k = c // LEVELS, c % LEVELS
        x[ch, k, pl.ds(PAD + rows, 1), :] = recv_r[0, pl.ds(2 * c, 1), :]
        x[ch, k, pl.ds(PAD - 1, 1), :] = recv_r[1, pl.ds(2 * c + 1, 1), :]
    for c in range(ENTRIES):
        slab_r[c, 2:4, :] = recv_r[0, pl.ds(2 * c, 2), :]
        slab_r[c, 4:6, :] = recv_r[1, pl.ds(2 * c, 2), :]

    def side_of(hold, c, val):
        ends = pltpu.roll(hold, (128 - (4 * c + 2)) % 128, 1)
        east = pltpu.roll(jnp.where(lane == 0, ends, val), 127, 1)
        west = pltpu.roll(jnp.where(lane == 127, ends, val), 1, 1)
        return east, west

    filler = jnp.zeros((128 - rows, 128), f32)
    own = jnp.concatenate([pack[...], filler], axis=0)
    half = (lax.broadcasted_iota(jnp.int32, (128, 128), 1) & 3) < 2
    east_t = jnp.transpose(jnp.where(half, own, ext[0]))
    west_t = jnp.transpose(jnp.where(half, ext[1], own))
    for c in range(ENTRIES):
        slab_c[c, 0:4, :] = east_t[4 * c : 4 * c + 4, :]
        slab_c[c, 4:8, :] = west_t[4 * c : 4 * c + 4, :]

    def slab_step(slab, east_west, north_south, keep):
        metrics = [slab[5 * LEVELS + m] for m in range(8)]
        f = [[slab[ch * LEVELS + k] for k in range(LEVELS)] for ch in range(5)]
        sums = None
        for k in range(LEVELS):
            now = [f[ch][k] for ch in range(5)]
            lower = [f[ch][k + 1] for ch in range(5)] if k < LEVELS - 1 else [None] * 5
            upper = [f[ch][k - 1] for ch in range(5)] if k > 0 else [None] * 5
            e, w = zip(*[east_west(ch * LEVELS + k, now[ch]) for ch in range(5)])
            n, s = zip(*[north_south(now[ch]) for ch in range(5)])
            cf = level_coefficients(k, now[WET], e[WET], w[WET], n[WET], s[WET], metrics, inv_h2, lower[WET], upper[WET])
            new, sums = advance_level(k, now, lower, upper, e, w, n, s, cf, heights, sums)
            for ch in range(4):
                keep(ch, k, new[ch])

    def along_rows(a):
        return pltpu.roll(a, 7, 0), pltpu.roll(a, 1, 0)

    def along_lanes(a):
        return pltpu.roll(a, 127, 1), pltpu.roll(a, 1, 1)

    z[...] = jnp.zeros((128, 128), f32)

    def keep_column(ch, k, val):
        c = ch * LEVELS + k
        z[pl.ds(4 * c + 1, 1), :] = val[5:6, :]
        z[pl.ds(4 * c + 2, 1), :] = val[2:3, :]

    slab_step(slab_c, lambda c, a: along_rows(a), along_lanes, keep_column)
    z[...] = jnp.transpose(z[...])

    is_east = (lane & 3) == 2
    far_n = jnp.where(is_east, ext[0, up, :], ext[1, up, :])[0:1, :]
    far_s = jnp.where(is_east, ext[0, down, :], ext[1, down, :])[7:8, :]
    far = jnp.where(sub == 2, jnp.broadcast_to(far_n, (8, 128)), jnp.broadcast_to(far_s, (8, 128)))

    def keep_row(ch, k, val):
        y[ch, k, pl.ds(PAD + rows, 1), :] = val[2:3, :]
        y[ch, k, pl.ds(PAD - 1, 1), :] = val[5:6, :]

    slab_step(slab_r, lambda c, a: side_of(far, c, a), along_rows, keep_row)

    def neighbours(src, r, k, hold, channels):
        def pick(ch, at, shift):
            return src[ch, at, pl.ds(PAD + 8 * r + shift, 8), :]

        now = [pick(ch, k, 0) for ch in range(channels)]
        lower = [pick(ch, k + 1, 0) for ch in range(channels)] if k < LEVELS - 1 else [None] * 5
        upper = [pick(ch, k - 1, 0) for ch in range(channels)] if k > 0 else [None] * 5
        e, w = zip(*[side_of(hold, ch * LEVELS + k, now[ch]) for ch in range(channels)])
        n = [pick(ch, k, 1) for ch in range(channels)]
        s = [pick(ch, k, -1) for ch in range(channels)]
        return now, lower, upper, e, w, n, s

    @pl.loop(0, chunks)
    def _(r):
        span = pl.ds(pl.multiple_of(8 * r, 8), 8)
        held = pl.ds(pl.multiple_of(PAD + 8 * r, 8), 8)
        hold = jnp.where(is_east, ext[0, span, :], ext[1, span, :])
        metrics = [metric(m, span) for m in range(8)]
        sums = None
        for k in range(LEVELS):
            now, lower, upper, e, w, n, s = neighbours(x, r, k, hold, 5)
            cf = level_coefficients(k, now[WET], e[WET], w[WET], n[WET], s[WET], metrics, inv_h2, lower[WET], upper[WET])
            new, sums = advance_level(k, now, lower, upper, e, w, n, s, cf, heights, sums)
            for i, val in enumerate(cf):
                if val is not None:
                    coef_s[i, k, span, :] = val
            for ch in range(4):
                y[ch, k, held, :] = new[ch]

    @pl.loop(0, chunks)
    def _(r):
        span = pl.ds(pl.multiple_of(8 * r, 8), 8)
        hold = z[span, :]
        sums = None
        for k in range(LEVELS):
            now, lower, upper, e, w, n, s = neighbours(y, r, k, hold, 4)
            absent = {9} if k == LEVELS - 1 else ({10} if k == 0 else set())
            cf = [None if i in absent else coef_s[i, k, span, :] for i in range(11)]
            new, sums = advance_level(k, now, lower, upper, e, w, n, s, cf, heights, sums)
            for ch in range(4):
                x4[ch, k, span, :] = new[ch]

    stores = [pltpu.make_async_copy(x4.at[c], outs[c], out_sem.at[c]) for c in range(4)]
    for store in stores:
        store.start()

    to_east.wait_send()
    to_west.wait_send()
    to_n.wait_send()

    @pl.when(ne_other)
    def _():
        to_ne.wait_send()

    @pl.when(nw_other)
    def _():
        to_nw.wait_send()

    @pl.when(inner)
    def _():
        to_s.wait_send()
        to_se.wait_send()
        to_sw.wait_send()

    for store in stores:
        store.wait()


def solution(mesh):
    nlon, nlat = mesh.shape["lon"], mesh.shape["lat"]

    def shards(*args):
        levels, rows, cols = args[0].shape
        f32 = jnp.float32
        vmem = pltpu.VMEM
        return tuple(pl.pallas_call(
            functools.partial(kernel, nlon, nlat, rows, cols),
            out_shape=[jax.ShapeDtypeStruct((levels, rows, cols), f32)] * 4,
            in_specs=[pl.BlockSpec(memory_space=pltpu.HBM)] * 11 + [pl.BlockSpec(memory_space=pltpu.SMEM)],
            out_specs=[pl.BlockSpec(memory_space=pltpu.HBM)] * 4,
            scratch_shapes=[
                vmem((4, levels, rows, cols), f32),
                vmem((levels, rows, cols), jnp.int32),
                vmem((rows, cols), jnp.int32),
                vmem((4, rows, cols), f32),
                vmem((levels - 1, rows, cols), f32),
                vmem((5, levels, rows + 2 * PAD, cols), f32),
                vmem((4, levels, rows + 2 * PAD, cols), f32),
                vmem((11, levels, rows, cols), f32),
                vmem((rows, 128), f32),
                vmem((2, 128, 128), f32),
                vmem((2, 2 * ENTRIES, cols), f32),
                vmem((2, 2 * ENTRIES, cols), f32),
                vmem((8, 128), f32),
                vmem((ENTRIES, 8, 128), f32),
                vmem((ENTRIES, 8, cols), f32),
                vmem((128, 128), f32),
                pltpu.SemaphoreType.DMA((11,)),
                pltpu.SemaphoreType.DMA((4,)),
                pltpu.SemaphoreType.DMA((8,)),
                pltpu.SemaphoreType.DMA((8,)),
            ],
            compiler_params=pltpu.CompilerParams(
                collective_id=0, has_side_effects=True, vmem_limit_bytes=60 * 1024 * 1024
            ),
        )(*args))

    field, plane = P(None, "lat", "lon"), P("lat", "lon")
    return jax.shard_map(
        shards,
        mesh=mesh,
        in_specs=(field,) * 5 + (plane,) * 5 + (field, P()),
        out_specs=(field,) * 4,
        check_vma=False,
    )
```

```python
import functools

import jax
import jax.numpy as jnp
from jax import lax
from jax.experimental import pallas as pl
from jax.experimental.pallas import tpu as pltpu
from jax.sharding import PartitionSpec as P

MESH = pl.DeviceIdType.MESH
TIME_STEP = 0.25
EXPANSION = 0.2
CONTRACTION = 0.8
BOTTOM_DRAG = 1.0
LEVELS = 4
ENTRIES = 28
FIELDS = 16
WET = 4
PAD = 8


def placed(c):
    if 8 <= c < 12:
        return c + 4
    if 12 <= c < 16:
        return c - 4
    return {21: 22, 22: 21}.get(c, c)


def kernel(nlon, nlat, rows, cols, *refs):
    ins, h_ref = refs[:11], refs[11]
    outs = refs[12:16]
    (st, hold, wet_i, floor_i, pack, ext, send_r, recv_r, corner, z, in_sem, out_sem, s_sem, r_sem) = refs[16:]
    lon, lat = lax.axis_index("lon"), lax.axis_index("lat")
    top, bottom = lat == nlat - 1, lat == 0
    topi = top.astype(jnp.int32)
    f32 = jnp.float32
    chunks = rows // 8
    row_tile, col_tile = chunks, chunks + 1
    row0, col0 = PAD + 8 * (chunks + 1), PAD + 8 * (chunks + 2)
    body = pl.ds(PAD, rows)

    wet0, met0 = 2 * FIELDS, 2 * FIELDS + LEVELS
    loads = [pltpu.make_async_copy(ins[c], st.at[pl.ds(4 * c, 4), body], in_sem.at[c]) for c in range(4)]
    loads.append(pltpu.make_async_copy(ins[4], wet_i, in_sem.at[4]))
    loads.append(pltpu.make_async_copy(ins[5], floor_i, in_sem.at[5]))
    loads += [pltpu.make_async_copy(ins[6 + m], st.at[met0 + 1 + m, body], in_sem.at[6 + m]) for m in range(4)]
    loads.append(pltpu.make_async_copy(ins[10], st.at[pl.ds(met0 + 5, 3), body], in_sem.at[10]))
    for load in loads:
        load.start()

    e_lon, w_lon = lax.rem(lon + 1, nlon), lax.rem(lon + nlon - 1, nlon)
    n_lat = jnp.where(top, lat, lat + 1)
    n_lon = jnp.where(top, nlon - 1 - lon, lon)
    ne_lon = jnp.where(top, lax.rem(2 * nlon - 2 - lon, nlon), e_lon)
    nw_lon = jnp.where(top, lax.rem(nlon - lon, nlon), w_lon)
    s_lat = jnp.maximum(lat - 1, 0)
    ne_self = jnp.logical_and(top, ne_lon == lon)
    nw_self = jnp.logical_and(top, nw_lon == lon)
    ne_other = jnp.logical_not(ne_self)
    nw_other = jnp.logical_not(nw_self)
    inner = jnp.logical_not(bottom)

    @pl.when(bottom)
    def _():
        ext[0, 120:, :] = jnp.zeros((8, 128), f32)
        ext[1, 120:, :] = jnp.zeros((8, 128), f32)
        recv_r[1, : 2 * 5 * LEVELS, :] = jnp.zeros((2 * 5 * LEVELS, cols), f32)
        recv_r[1, 2 * 5 * LEVELS :, :] = jnp.ones((2 * ENTRIES - 10 * LEVELS, cols), f32)

    barrier = pltpu.get_barrier_semaphore()

    def greet(dev):
        pl.semaphore_signal(barrier, inc=1, device_id=dev, device_id_type=MESH)

    greet((e_lon, lat))
    greet((w_lon, lat))
    greet((n_lon, n_lat))

    @pl.when(ne_other)
    def _():
        greet((ne_lon, n_lat))

    @pl.when(nw_other)
    def _():
        greet((nw_lon, n_lat))

    @pl.when(inner)
    def _():
        greet((lon, s_lat))
        greet((e_lon, s_lat))
        greet((w_lon, s_lat))

    lane = lax.broadcasted_iota(jnp.int32, (8, 128), 1)
    sub = lax.broadcasted_iota(jnp.int32, (8, 128), 0)
    heights = [jnp.full((8, 128), h_ref[k], f32) for k in range(LEVELS)]
    inv_h2 = [1.0 / (h * h) for h in heights]

    for load in loads:
        load.wait()

    group = lane >> 2

    @pl.loop(0, chunks)
    def _(r):
        span = pl.ds(pl.multiple_of(8 * r, 8), 8)
        held = pl.ds(pl.multiple_of(PAD + 8 * r, 8), 8)
        packed = jnp.zeros((8, 128), f32)
        wet = [wet_i[k, span, :].astype(f32) for k in range(LEVELS)]
        for c in range(ENTRIES):
            ch, k = c // LEVELS, c % LEVELS
            at = c if ch < WET else c + FIELDS
            if ch < WET:
                val = st[at, held, :] * wet[k]
            elif ch == WET:
                val = wet[k]
            elif at == met0:
                val = floor_i[span, :].astype(f32)
            else:
                val = st[at, held, :]
            if at <= met0:
                st[at, held, :] = val
            g = placed(c)
            packed = jnp.where(group == g, pltpu.roll(val, (4 * g + 2) % 128, 1), packed)
        pack[span, :] = packed

    def entries(fn):
        @pl.loop(0, ENTRIES // 4)
        def _(g):
            for i in range(4):
                c = 4 * g + i
                fn(c, c + FIELDS * (g >= FIELDS // 4).astype(jnp.int32))

    def edge_rows(c, at):
        low, high = st[at, pl.ds(PAD, 2), :], st[at, pl.ds(PAD + rows - 2, 2), :]
        send_r[1, pl.ds(2 * c, 2), :] = low
        send_r[0, pl.ds(2 * c, 2), :] = high
        st[at, pl.ds(row0, 2), :] = high
        st[at, pl.ds(row0 + 6, 2), :] = low

    entries(edge_rows)

    @pl.when(top)
    def _():
        @pl.loop(0, 2 * ENTRIES // 8)
        def _(t):
            span = pl.ds(pl.multiple_of(8 * t, 8), 8)
            val = send_r[0, span, :]
            val = jnp.where((sub & 1) == 1, pltpu.roll(val, 1, 0), pltpu.roll(val, 7, 0))
            step = 1
            while step < cols:
                val = jnp.where((lane & step) != 0, pltpu.roll(val, step, 1), pltpu.roll(val, cols - step, 1))
                step *= 2
            flipped = jnp.logical_and(8 * t + sub >= 4 * LEVELS, 8 * t + sub < 8 * LEVELS)
            send_r[0, span, :] = jnp.where(flipped, -val, val)

    last = pack[pl.ds(rows - 8, 8), :]
    turned = jnp.broadcast_to(last[7:8, :], (8, 128))
    for step in (1, 2):
        turned = jnp.where((lane & step) != 0, pltpu.roll(turned, step, 1), pltpu.roll(turned, 128 - step, 1))
    turned = jnp.where(jnp.logical_and(lane >= 8 * LEVELS, lane < 16 * LEVELS), -turned, turned)
    top_v = jnp.full((8, 128), topi) == 1
    folded = jnp.where(top_v, turned, last)
    corner[...] = folded

    @pl.when(ne_self)
    def _():
        ext[0, pl.ds(rows, 8), :] = folded

    @pl.when(nw_self)
    def _():
        ext[1, pl.ds(rows, 8), :] = folded

    pl.semaphore_wait(
        barrier,
        3 + ne_other.astype(jnp.int32) + nw_other.astype(jnp.int32) + 3 * inner.astype(jnp.int32),
    )

    def copy(src, dst, s, r, dev):
        return pltpu.make_async_remote_copy(
            src_ref=src, dst_ref=dst, send_sem=s_sem.at[s], recv_sem=r_sem.at[r], device_id=dev, device_id_type=MESH
        )

    whole, up, down = pl.ds(0, rows), pl.ds(rows, 8), pl.ds(120, 8)
    over = pl.ds(pl.multiple_of(120 - (120 - rows) * topi, 8), 8)
    to_east = copy(pack.at[whole], ext.at[1, whole], 0, 1, (e_lon, lat))
    to_west = copy(pack.at[whole], ext.at[0, whole], 1, 0, (w_lon, lat))
    to_n = copy(send_r.at[0], recv_r.at[1 - topi], 2, 3 - topi, (n_lon, n_lat))
    to_ne = copy(corner, ext.at[1 - topi, over], 4, 7 - 3 * topi, (ne_lon, n_lat))
    to_nw = copy(corner, ext.at[topi, over], 5, 6 - topi, (nw_lon, n_lat))
    to_s = copy(send_r.at[1], recv_r.at[0], 3, 2, (lon, s_lat))
    to_se = copy(pack.at[pl.ds(0, 8)], ext.at[1, up], 6, 5, (e_lon, s_lat))
    to_sw = copy(pack.at[pl.ds(0, 8)], ext.at[0, up], 7, 4, (w_lon, s_lat))
    from_s = copy(send_r.at[0], recv_r.at[1], 2, 3, (lon, s_lat))
    from_se = copy(corner, ext.at[0, down], 5, 6, (e_lon, s_lat))
    from_sw = copy(corner, ext.at[1, down], 4, 7, (w_lon, s_lat))

    to_n.start()
    to_east.start()
    to_west.start()

    @pl.when(ne_other)
    def _():
        to_ne.start()

    @pl.when(nw_other)
    def _():
        to_nw.start()

    @pl.when(inner)
    def _():
        to_s.start()
        to_se.start()
        to_sw.start()

    to_s.wait_recv()

    @pl.when(inner)
    def _():
        from_s.wait_recv()
        from_se.wait_recv()
        from_sw.wait_recv()

    @pl.when(ne_other)
    def _():
        to_sw.wait_recv()

    @pl.when(nw_other)
    def _():
        to_se.wait_recv()

    to_west.wait_recv()
    to_east.wait_recv()

    pair = (lax.broadcasted_iota(jnp.int32, (128, 128), 1) >> 1) & 1

    @pl.loop(0, 2)
    def _(side):
        z[side] = jnp.transpose(jnp.where(pair != side, ext[side], pack[...]))

    def gather(c, at):
        north, south = recv_r[0, pl.ds(2 * c, 2), :], recv_r[1, pl.ds(2 * c, 2), :]
        st[at, pl.ds(PAD + rows, 1), :] = north[0:1, :]
        st[at, pl.ds(PAD - 1, 1), :] = south[1:2, :]
        st[at, pl.ds(row0 + 2, 2), :] = north
        st[at, pl.ds(row0 + 4, 2), :] = south
        st[at, pl.ds(col0, 4), :] = z[0, pl.ds(4 * c, 4), :]
        st[at, pl.ds(col0 + 4, 4), :] = z[1, pl.ds(4 * c, 4), :]

    entries(gather)
    st[met0 + 3, pl.ds(col0, 8), :] = -st[met0 + 3, pl.ds(col0, 8), :]

    is_east = (lane & 3) == 2

    @pl.loop(0, chunks)
    def _(r):
        span = pl.ds(pl.multiple_of(8 * r, 8), 8)
        hold[0, pl.ds(pl.multiple_of(PAD + 8 * r, 8), 8), :] = jnp.where(is_east, ext[0, span, :], ext[1, span, :])

    far_n = jnp.where(is_east, ext[0, up, :], ext[1, up, :])[0:1, :]
    far_s = jnp.where(is_east, ext[0, down, :], ext[1, down, :])[7:8, :]
    hold[0, pl.ds(row0, 8), :] = jnp.where(
        sub == 2, jnp.broadcast_to(far_n, (8, 128)), jnp.broadcast_to(far_s, (8, 128))
    )

    def between():
        @pl.loop(0, 5 * LEVELS // 4)
        def _(g):
            for i in range(4):
                c = 4 * g + i
                at = FIELDS + c
                st[at, pl.ds(PAD + rows, 1), :] = st[at, pl.ds(row0 + 2, 1), :]
                st[at, pl.ds(PAD - 1, 1), :] = st[at, pl.ds(row0 + 5, 1), :]
                z[0, pl.ds(4 * c + 2, 1), :] = st[at, pl.ds(col0 + 2, 1), :]
                z[0, pl.ds(4 * c + 1, 1), :] = st[at, pl.ds(col0 + 5, 1), :]

        hold[1, body, :] = jnp.transpose(z[0])[:rows, :]

    first_step = chunks + 2

    @pl.loop(0, first_step + chunks)
    def _(t):
        pl.when(t == first_step)(between)
        second = (t >= first_step).astype(jnp.int32)
        tile = t - first_step * second
        off = pl.multiple_of(PAD + 8 * (tile + (tile >= chunks).astype(jnp.int32)), 8)
        held = pl.ds(off, 8)
        src = FIELDS * second
        dst = FIELDS - src
        turned_tile = (tile == col_tile).astype(jnp.int32)
        at_first = lane == 0 - turned_tile
        at_last = lane == 127 + turned_tile
        ends_all = hold[second, held, :]

        def side_of(c, val):
            ends = pltpu.roll(ends_all, (126 - 4 * placed(c)) % 128, 1)
            east = pltpu.roll(jnp.where(at_first, ends, val), 127, 1)
            west = pltpu.roll(jnp.where(at_last, ends, val), 1, 1)
            return east, west

        def around(c, at):
            val = st[at, held, :]
            return (val, *side_of(c, val), st[at, pl.ds(off + 1, 8), :], st[at, pl.ds(off - 1, 8), :])

        floor, zs, ms, rot, eddy, *mix = [st[met0 + m, held, :] for m in range(8)]
        rz, rm = 1.0 / zs, 1.0 / ms
        kx, ky, hx, hy = eddy * rz * rz, eddy * rm * rm, 0.5 * rz, 0.5 * rm
        sum_x = sum_y = None
        for k in range(LEVELS):
            wet, we, ww, wn, ws = around(WET * LEVELS + k, wet0 + k)
            dtw = TIME_STEP * wet
            ax, ay = dtw * kx, dtw * ky
            bx, by, br = dtw * hx, dtw * hy, dtw * rot
            ae, aw, an, as_ = ax * we, ax * ww, ay * wn, ay * ws
            centre = 1.0 - (ae + aw) - (an + as_)
            t2 = dtw * inv_h2[k]
            below = above = None
            if k < LEVELS - 1:
                below = t2 * mix[k] * st[wet0 + k + 1, held, :]
                centre = centre - below
            if k > 0:
                above = t2 * mix[k - 1] * st[wet0 + k - 1, held, :]
                centre = centre - above
            drag = centre - jnp.where(floor == float(k), BOTTOM_DRAG * dtw, 0.0)
            u, v = st[src + 2 * LEVELS + k, held, :], st[src + 3 * LEVELS + k, held, :]
            bu, bv = bx * u, by * v
            ce, cw, cn, cs = ae - bu, aw + bu, an - bv, as_ + bv
            layer_x = layer_y = None
            for ch in range(4):
                c = ch * LEVELS + k
                val, east, west, north, south = around(c, src + c)
                new = (centre if ch < 2 else drag) * val + (ce * east + cw * west) + (cn * north + cs * south)
                if below is not None:
                    new = new + below * st[src + c + 1, held, :]
                if above is not None:
                    new = new + above * st[src + c - 1, held, :]
                if ch == 0:
                    layer_x, layer_y = EXPANSION * (west - east), EXPANSION * (south - north)
                if ch == 1:
                    layer_x = (layer_x + CONTRACTION * (east - west)) * heights[k]
                    layer_y = (layer_y + CONTRACTION * (north - south)) * heights[k]
                    sum_x = layer_x if k == 0 else sum_x + layer_x
                    sum_y = layer_y if k == 0 else sum_y + layer_y
                if ch == 2:
                    new = new + br * v - bx * (sum_x - 0.5 * layer_x)
                if ch == 3:
                    new = new - br * u - by * (sum_y - 0.5 * layer_y)
                st[dst + c, held, :] = new

    stores = [pltpu.make_async_copy(st.at[pl.ds(4 * c, 4), body], outs[c], out_sem.at[c]) for c in range(4)]
    for store in stores:
        store.start()

    to_east.wait_send()
    to_west.wait_send()
    to_n.wait_send()

    @pl.when(ne_other)
    def _():
        to_ne.wait_send()

    @pl.when(nw_other)
    def _():
        to_nw.wait_send()

    @pl.when(inner)
    def _():
        to_s.wait_send()
        to_se.wait_send()
        to_sw.wait_send()

    for store in stores:
        store.wait()


def hand_over(*refs):
    moves = []
    for c in range(4):
        for half in range(2):
            part = pl.ds(2 * half, 2)
            moves.append(pltpu.make_async_copy(refs[c].at[part], refs[4 + c].at[part], refs[8].at[2 * c + half]))
    for move in moves:
        move.start()
    for move in moves:
        move.wait()


def solution(mesh):
    nlon, nlat = mesh.shape["lon"], mesh.shape["lat"]

    def shards(*args):
        levels, rows, cols = args[0].shape
        f32 = jnp.float32
        vmem = pltpu.VMEM
        held = rows + 5 * PAD
        hbm = pl.BlockSpec(memory_space=pltpu.HBM)
        out_shape = [jax.ShapeDtypeStruct((levels, rows, cols), f32)] * 4
        results = pl.pallas_call(
            functools.partial(kernel, nlon, nlat, rows, cols),
            out_shape=out_shape,
            in_specs=[hbm] * 11 + [pl.BlockSpec(memory_space=pltpu.SMEM)],
            out_specs=[hbm] * 4,
            scratch_shapes=[
                vmem((2 * FIELDS + ENTRIES - FIELDS, held, cols), f32),
                vmem((2, held, 128), f32),
                vmem((levels, rows, cols), jnp.int32),
                vmem((rows, cols), jnp.int32),
                vmem((128, 128), f32),
                vmem((2, 128, 128), f32),
                vmem((2, 2 * ENTRIES, cols), f32),
                vmem((2, 2 * ENTRIES, cols), f32),
                vmem((8, 128), f32),
                vmem((2, 128, 128), f32),
                pltpu.SemaphoreType.DMA((11,)),
                pltpu.SemaphoreType.DMA((4,)),
                pltpu.SemaphoreType.DMA((8,)),
                pltpu.SemaphoreType.DMA((8,)),
            ],
            compiler_params=pltpu.CompilerParams(
                collective_id=0, has_side_effects=True, vmem_limit_bytes=60 * 1024 * 1024
            ),
        )(*args)
        return tuple(pl.pallas_call(
            hand_over,
            out_shape=out_shape,
            in_specs=[hbm] * 4,
            out_specs=[hbm] * 4,
            scratch_shapes=[pltpu.SemaphoreType.DMA((8,))],
            compiler_params=pltpu.CompilerParams(vmem_limit_bytes=60 * 1024 * 1024),
        )(*results))

    field, plane = P(None, "lat", "lon"), P("lat", "lon")
    return jax.shard_map(
        shards,
        mesh=mesh,
        in_specs=(field,) * 5 + (plane,) * 5 + (field, P()),
        out_specs=(field,) * 4,
        check_vma=False,
    )
```

```python
import functools

import jax
import jax.numpy as jnp
from jax import lax
from jax.experimental import pallas as pl
from jax.experimental.pallas import tpu as pltpu
from jax.sharding import PartitionSpec as P

MESH = pl.DeviceIdType.MESH
TIME_STEP = 0.25
EXPANSION = 0.2
CONTRACTION = 0.8
BOTTOM_DRAG = 1.0
LEVELS = 4
ENTRIES = 28
FIELDS = 16
WET = 4
PAD = 8


def placed(c):
    if 8 <= c < 12:
        return c + 4
    if 12 <= c < 16:
        return c - 4
    return {21: 22, 22: 21}.get(c, c)


def kernel(nlon, nlat, rows, cols, *refs):
    ins, h_ref = refs[:11], refs[11]
    outs = refs[12:16]
    (st, hold, wet_i, floor_i, pack, ext, send_r, recv_r, corner, z, in_sem, out_sem, s_sem, r_sem) = refs[16:]
    lon, lat = lax.axis_index("lon"), lax.axis_index("lat")
    top, bottom = lat == nlat - 1, lat == 0
    topi = top.astype(jnp.int32)
    f32 = jnp.float32
    chunks = rows // 8
    row_tile, col_tile = chunks, chunks + 1
    row0, col0 = PAD + 8 * (chunks + 1), PAD + 8 * (chunks + 2)
    body = pl.ds(PAD, rows)

    wet0, met0 = 2 * FIELDS, 2 * FIELDS + LEVELS
    loads = [pltpu.make_async_copy(ins[c], st.at[pl.ds(4 * c, 4), body], in_sem.at[c]) for c in range(4)]
    loads.append(pltpu.make_async_copy(ins[4], wet_i, in_sem.at[4]))
    loads.append(pltpu.make_async_copy(ins[5], floor_i, in_sem.at[5]))
    loads += [pltpu.make_async_copy(ins[6 + m], st.at[met0 + 1 + m, body], in_sem.at[6 + m]) for m in range(4)]
    loads.append(pltpu.make_async_copy(ins[10], st.at[pl.ds(met0 + 5, 3), body], in_sem.at[10]))
    for load in loads:
        load.start()

    e_lon, w_lon = lax.rem(lon + 1, nlon), lax.rem(lon + nlon - 1, nlon)
    n_lat = jnp.where(top, lat, lat + 1)
    n_lon = jnp.where(top, nlon - 1 - lon, lon)
    ne_lon = jnp.where(top, lax.rem(2 * nlon - 2 - lon, nlon), e_lon)
    nw_lon = jnp.where(top, lax.rem(nlon - lon, nlon), w_lon)
    s_lat = jnp.maximum(lat - 1, 0)
    ne_self = jnp.logical_and(top, ne_lon == lon)
    nw_self = jnp.logical_and(top, nw_lon == lon)
    ne_other = jnp.logical_not(ne_self)
    nw_other = jnp.logical_not(nw_self)
    inner = jnp.logical_not(bottom)

    @pl.when(bottom)
    def _():
        ext[0, 120:, :] = jnp.zeros((8, 128), f32)
        ext[1, 120:, :] = jnp.zeros((8, 128), f32)
        recv_r[1, : 2 * 5 * LEVELS, :] = jnp.zeros((2 * 5 * LEVELS, cols), f32)
        recv_r[1, 2 * 5 * LEVELS :, :] = jnp.ones((2 * ENTRIES - 10 * LEVELS, cols), f32)

    barrier = pltpu.get_barrier_semaphore()

    def greet(dev):
        pl.semaphore_signal(barrier, inc=1, device_id=dev, device_id_type=MESH)

    greet((e_lon, lat))
    greet((w_lon, lat))
    greet((n_lon, n_lat))

    @pl.when(ne_other)
    def _():
        greet((ne_lon, n_lat))

    @pl.when(nw_other)
    def _():
        greet((nw_lon, n_lat))

    @pl.when(inner)
    def _():
        greet((lon, s_lat))
        greet((e_lon, s_lat))
        greet((w_lon, s_lat))

    lane = lax.broadcasted_iota(jnp.int32, (8, 128), 1)
    sub = lax.broadcasted_iota(jnp.int32, (8, 128), 0)
    heights = [jnp.full((8, 128), h_ref[k], f32) for k in range(LEVELS)]
    inv_h2 = [1.0 / (h * h) for h in heights]

    for load in loads:
        load.wait()

    group = lane >> 2

    @pl.loop(0, chunks)
    def _(r):
        span = pl.ds(pl.multiple_of(8 * r, 8), 8)
        held = pl.ds(pl.multiple_of(PAD + 8 * r, 8), 8)
        packed = jnp.zeros((8, 128), f32)
        kept = []
        wet = [wet_i[k, span, :].astype(f32) for k in range(LEVELS)]
        for c in range(ENTRIES):
            ch, k = c // LEVELS, c % LEVELS
            at = c if ch < WET else c + FIELDS
            if ch < WET:
                val = st[at, held, :] * wet[k]
            elif ch == WET:
                val = wet[k]
            elif at == met0:
                val = floor_i[span, :].astype(f32)
            else:
                val = st[at, held, :]
            if at <= met0:
                kept.append((at, val))
            g = placed(c)
            packed = jnp.where(group == g, pltpu.roll(val, (4 * g + 2) % 128, 1), packed)
        pack[span, :] = packed
        for at, val in kept:
            st[at, held, :] = val

    def entries(load, save):
        @pl.loop(0, ENTRIES // 4)
        def _(g):
            at = 4 * g + FIELDS * (g >= FIELDS // 4).astype(jnp.int32)
            held = [load(4 * g + i, at + i) for i in range(4)]
            for i in range(4):
                save(4 * g + i, at + i, *held[i])

    def take_edges(c, at):
        return st[at, pl.ds(PAD, 2), :], st[at, pl.ds(PAD + rows - 2, 2), :]

    def put_edges(c, at, low, high):
        send_r[1, pl.ds(2 * c, 2), :] = low
        send_r[0, pl.ds(2 * c, 2), :] = high
        st[at, pl.ds(row0, 2), :] = high
        st[at, pl.ds(row0 + 6, 2), :] = low

    entries(take_edges, put_edges)

    @pl.when(top)
    def _():
        @pl.loop(0, 2 * ENTRIES // 8)
        def _(t):
            span = pl.ds(pl.multiple_of(8 * t, 8), 8)
            val = send_r[0, span, :]
            val = jnp.where((sub & 1) == 1, pltpu.roll(val, 1, 0), pltpu.roll(val, 7, 0))
            step = 1
            while step < cols:
                val = jnp.where((lane & step) != 0, pltpu.roll(val, step, 1), pltpu.roll(val, cols - step, 1))
                step *= 2
            flipped = jnp.logical_and(8 * t + sub >= 4 * LEVELS, 8 * t + sub < 8 * LEVELS)
            send_r[0, span, :] = jnp.where(flipped, -val, val)

    last = pack[pl.ds(rows - 8, 8), :]
    turned = jnp.broadcast_to(last[7:8, :], (8, 128))
    for step in (1, 2):
        turned = jnp.where((lane & step) != 0, pltpu.roll(turned, step, 1), pltpu.roll(turned, 128 - step, 1))
    turned = jnp.where(jnp.logical_and(lane >= 8 * LEVELS, lane < 16 * LEVELS), -turned, turned)
    top_v = jnp.full((8, 128), topi) == 1
    folded = jnp.where(top_v, turned, last)
    corner[...] = folded

    @pl.when(ne_self)
    def _():
        ext[0, pl.ds(rows, 8), :] = folded

    @pl.when(nw_self)
    def _():
        ext[1, pl.ds(rows, 8), :] = folded

    pl.semaphore_wait(
        barrier,
        3 + ne_other.astype(jnp.int32) + nw_other.astype(jnp.int32) + 3 * inner.astype(jnp.int32),
    )

    def copy(src, dst, s, r, dev):
        return pltpu.make_async_remote_copy(
            src_ref=src, dst_ref=dst, send_sem=s_sem.at[s], recv_sem=r_sem.at[r], device_id=dev, device_id_type=MESH
        )

    whole, up, down = pl.ds(0, rows), pl.ds(rows, 8), pl.ds(120, 8)
    over = pl.ds(pl.multiple_of(120 - (120 - rows) * topi, 8), 8)
    to_east = copy(pack.at[whole], ext.at[1, whole], 0, 1, (e_lon, lat))
    to_west = copy(pack.at[whole], ext.at[0, whole], 1, 0, (w_lon, lat))
    to_n = copy(send_r.at[0], recv_r.at[1 - topi], 2, 3 - topi, (n_lon, n_lat))
    to_ne = copy(corner, ext.at[1 - topi, over], 4, 7 - 3 * topi, (ne_lon, n_lat))
    to_nw = copy(corner, ext.at[topi, over], 5, 6 - topi, (nw_lon, n_lat))
    to_s = copy(send_r.at[1], recv_r.at[0], 3, 2, (lon, s_lat))
    to_se = copy(pack.at[pl.ds(0, 8)], ext.at[1, up], 6, 5, (e_lon, s_lat))
    to_sw = copy(pack.at[pl.ds(0, 8)], ext.at[0, up], 7, 4, (w_lon, s_lat))
    from_s = copy(send_r.at[0], recv_r.at[1], 2, 3, (lon, s_lat))
    from_se = copy(corner, ext.at[0, down], 5, 6, (e_lon, s_lat))
    from_sw = copy(corner, ext.at[1, down], 4, 7, (w_lon, s_lat))

    to_n.start()
    to_east.start()
    to_west.start()

    @pl.when(ne_other)
    def _():
        to_ne.start()

    @pl.when(nw_other)
    def _():
        to_nw.start()

    @pl.when(inner)
    def _():
        to_s.start()
        to_se.start()
        to_sw.start()

    to_s.wait_recv()

    @pl.when(inner)
    def _():
        from_s.wait_recv()
        from_se.wait_recv()
        from_sw.wait_recv()

    @pl.when(ne_other)
    def _():
        to_sw.wait_recv()

    @pl.when(nw_other)
    def _():
        to_se.wait_recv()

    to_west.wait_recv()
    to_east.wait_recv()

    pair = (lax.broadcasted_iota(jnp.int32, (128, 128), 1) >> 1) & 1

    @pl.loop(0, 2)
    def _(side):
        z[side] = jnp.transpose(jnp.where(pair != side, ext[side], pack[...]))

    def take_halo(c, at):
        two, four = pl.ds(2 * c, 2), pl.ds(4 * c, 4)
        return recv_r[0, two, :], recv_r[1, two, :], z[0, four, :], z[1, four, :]

    def put_halo(c, at, north, south, east, west):
        st[at, pl.ds(PAD + rows, 1), :] = north[0:1, :]
        st[at, pl.ds(PAD - 1, 1), :] = south[1:2, :]
        st[at, pl.ds(row0 + 2, 2), :] = north
        st[at, pl.ds(row0 + 4, 2), :] = south
        st[at, pl.ds(col0, 4), :] = east
        st[at, pl.ds(col0 + 4, 4), :] = west

    entries(take_halo, put_halo)
    st[met0 + 3, pl.ds(col0, 8), :] = -st[met0 + 3, pl.ds(col0, 8), :]

    is_east = (lane & 3) == 2

    @pl.loop(0, chunks)
    def _(r):
        span = pl.ds(pl.multiple_of(8 * r, 8), 8)
        hold[0, pl.ds(pl.multiple_of(PAD + 8 * r, 8), 8), :] = jnp.where(is_east, ext[0, span, :], ext[1, span, :])

    far_n = jnp.where(is_east, ext[0, up, :], ext[1, up, :])[0:1, :]
    far_s = jnp.where(is_east, ext[0, down, :], ext[1, down, :])[7:8, :]
    hold[0, pl.ds(row0, 8), :] = jnp.where(
        sub == 2, jnp.broadcast_to(far_n, (8, 128)), jnp.broadcast_to(far_s, (8, 128))
    )

    def between():
        @pl.loop(0, 5 * LEVELS // 4)
        def _(g):
            held = [(st[FIELDS + 4 * g + i, pl.ds(row0, 8), :], st[FIELDS + 4 * g + i, pl.ds(col0, 8), :]) for i in range(4)]
            for i, (about_row, about_col) in enumerate(held):
                c = 4 * g + i
                st[FIELDS + c, pl.ds(PAD + rows, 1), :] = about_row[2:3, :]
                st[FIELDS + c, pl.ds(PAD - 1, 1), :] = about_row[5:6, :]
                z[0, pl.ds(4 * c + 2, 1), :] = about_col[2:3, :]
                z[0, pl.ds(4 * c + 1, 1), :] = about_col[5:6, :]

        hold[1, body, :] = jnp.transpose(z[0])[:rows, :]

    first_step = chunks + 2

    @pl.loop(0, first_step + chunks)
    def _(t):
        pl.when(t == first_step)(between)
        second = (t >= first_step).astype(jnp.int32)
        tile = t - first_step * second
        off = pl.multiple_of(PAD + 8 * (tile + (tile >= chunks).astype(jnp.int32)), 8)
        held = pl.ds(off, 8)
        src = FIELDS * second
        dst = FIELDS - src
        turned_tile = (tile == col_tile).astype(jnp.int32)
        at_first = lane == 0 - turned_tile
        at_last = lane == 127 + turned_tile
        ends_all = hold[second, held, :]

        def side_of(c, val):
            ends = pltpu.roll(ends_all, (126 - 4 * placed(c)) % 128, 1)
            east = pltpu.roll(jnp.where(at_first, ends, val), 127, 1)
            west = pltpu.roll(jnp.where(at_last, ends, val), 1, 1)
            return east, west

        def around(c, at):
            val = st[at, held, :]
            return (val, *side_of(c, val), st[at, pl.ds(off + 1, 8), :], st[at, pl.ds(off - 1, 8), :])

        floor, zs, ms, rot, eddy, *mix = [st[met0 + m, held, :] for m in range(8)]
        rz, rm = 1.0 / zs, 1.0 / ms
        kx, ky, hx, hy = eddy * rz * rz, eddy * rm * rm, 0.5 * rz, 0.5 * rm
        results = []
        sum_x = sum_y = None
        for k in range(LEVELS):
            wet, we, ww, wn, ws = around(WET * LEVELS + k, wet0 + k)
            dtw = TIME_STEP * wet
            ax, ay = dtw * kx, dtw * ky
            bx, by, br = dtw * hx, dtw * hy, dtw * rot
            ae, aw, an, as_ = ax * we, ax * ww, ay * wn, ay * ws
            centre = 1.0 - (ae + aw) - (an + as_)
            t2 = dtw * inv_h2[k]
            below = above = None
            if k < LEVELS - 1:
                below = t2 * mix[k] * st[wet0 + k + 1, held, :]
                centre = centre - below
            if k > 0:
                above = t2 * mix[k - 1] * st[wet0 + k - 1, held, :]
                centre = centre - above
            drag = centre - jnp.where(floor == float(k), BOTTOM_DRAG * dtw, 0.0)
            u, v = st[src + 2 * LEVELS + k, held, :], st[src + 3 * LEVELS + k, held, :]
            bu, bv = bx * u, by * v
            ce, cw, cn, cs = ae - bu, aw + bu, an - bv, as_ + bv
            layer_x = layer_y = None
            for ch in range(4):
                c = ch * LEVELS + k
                val, east, west, north, south = around(c, src + c)
                new = (centre if ch < 2 else drag) * val + (ce * east + cw * west) + (cn * north + cs * south)
                if below is not None:
                    new = new + below * st[src + c + 1, held, :]
                if above is not None:
                    new = new + above * st[src + c - 1, held, :]
                if ch == 0:
                    layer_x, layer_y = EXPANSION * (west - east), EXPANSION * (south - north)
                if ch == 1:
                    layer_x = (layer_x + CONTRACTION * (east - west)) * heights[k]
                    layer_y = (layer_y + CONTRACTION * (north - south)) * heights[k]
                    sum_x = layer_x if k == 0 else sum_x + layer_x
                    sum_y = layer_y if k == 0 else sum_y + layer_y
                if ch == 2:
                    new = new + br * v - bx * (sum_x - 0.5 * layer_x)
                if ch == 3:
                    new = new - br * u - by * (sum_y - 0.5 * layer_y)
                results.append((c, new))
        for c, new in results:
            st[dst + c, held, :] = new

    stores = [pltpu.make_async_copy(st.at[pl.ds(4 * c, 4), body], outs[c], out_sem.at[c]) for c in range(4)]
    for store in stores:
        store.start()

    to_east.wait_send()
    to_west.wait_send()
    to_n.wait_send()

    @pl.when(ne_other)
    def _():
        to_ne.wait_send()

    @pl.when(nw_other)
    def _():
        to_nw.wait_send()

    @pl.when(inner)
    def _():
        to_s.wait_send()
        to_se.wait_send()
        to_sw.wait_send()

    for store in stores:
        store.wait()


def hand_over(*refs):
    held, sem_in, sem_out = refs[8:]
    moves = [pltpu.make_async_copy(refs[c], held.at[c], sem_in.at[c]) for c in range(4)]
    stores = [pltpu.make_async_copy(held.at[c], refs[4 + c], sem_out.at[c]) for c in range(4)]
    for move in moves:
        move.start()
    for move, store in zip(moves, stores):
        move.wait()
        store.start()
    for store in stores:
        store.wait()


def solution(mesh):
    nlon, nlat = mesh.shape["lon"], mesh.shape["lat"]

    def shards(*args):
        levels, rows, cols = args[0].shape
        f32 = jnp.float32
        vmem = pltpu.VMEM
        held = rows + 5 * PAD
        hbm = pl.BlockSpec(memory_space=pltpu.HBM)
        out_shape = [jax.ShapeDtypeStruct((levels, rows, cols), f32)] * 4
        results = pl.pallas_call(
            functools.partial(kernel, nlon, nlat, rows, cols),
            out_shape=out_shape,
            in_specs=[hbm] * 11 + [pl.BlockSpec(memory_space=pltpu.SMEM)],
            out_specs=[hbm] * 4,
            scratch_shapes=[
                vmem((2 * FIELDS + ENTRIES - FIELDS, held, cols), f32),
                vmem((2, held, 128), f32),
                vmem((levels, rows, cols), jnp.int32),
                vmem((rows, cols), jnp.int32),
                vmem((128, 128), f32),
                vmem((2, 128, 128), f32),
                vmem((2, 2 * ENTRIES, cols), f32),
                vmem((2, 2 * ENTRIES, cols), f32),
                vmem((8, 128), f32),
                vmem((2, 128, 128), f32),
                pltpu.SemaphoreType.DMA((11,)),
                pltpu.SemaphoreType.DMA((4,)),
                pltpu.SemaphoreType.DMA((8,)),
                pltpu.SemaphoreType.DMA((8,)),
            ],
            compiler_params=pltpu.CompilerParams(
                collective_id=0, has_side_effects=True, vmem_limit_bytes=60 * 1024 * 1024
            ),
        )(*args)
        return tuple(pl.pallas_call(
            hand_over,
            out_shape=out_shape,
            in_specs=[hbm] * 4,
            out_specs=[hbm] * 4,
            scratch_shapes=[vmem((4, levels, rows, cols), f32), pltpu.SemaphoreType.DMA((4,)), pltpu.SemaphoreType.DMA((4,))],
            compiler_params=pltpu.CompilerParams(vmem_limit_bytes=60 * 1024 * 1024),
        )(*results))

    field, plane = P(None, "lat", "lon"), P("lat", "lon")
    return jax.shard_map(
        shards,
        mesh=mesh,
        in_specs=(field,) * 5 + (plane,) * 5 + (field, P()),
        out_specs=(field,) * 4,
        check_vma=False,
    )
```

```python
import functools

import jax
import jax.numpy as jnp
from jax import lax
from jax.experimental import pallas as pl
from jax.experimental.pallas import tpu as pltpu
from jax.sharding import PartitionSpec as P

MESH = pl.DeviceIdType.MESH
TIME_STEP = 0.25
EXPANSION = 0.2
CONTRACTION = 0.8
BOTTOM_DRAG = 1.0
LEVELS = 4
ENTRIES = 28
FIELDS = 16
WET = 4
PAD = 8


def placed(c):
    if 8 <= c < 12:
        return c + 4
    if 12 <= c < 16:
        return c - 4
    return {21: 22, 22: 21}.get(c, c)


def kernel(nlon, nlat, rows, cols, *refs):
    ins, h_ref = refs[:11], refs[11]
    outs = refs[12:16]
    (st, hold, wet_i, floor_i, pack, ext, send_r, recv_r, corner, z, in_sem, out_sem, s_sem, r_sem) = refs[16:]
    lon, lat = lax.axis_index("lon"), lax.axis_index("lat")
    top, bottom = lat == nlat - 1, lat == 0
    topi = top.astype(jnp.int32)
    f32 = jnp.float32
    chunks = rows // 8
    row_tile, col_tile = chunks, chunks + 1
    row0, col0 = PAD + 8 * (chunks + 1), PAD + 8 * (chunks + 2)
    body = pl.ds(PAD, rows)

    wet0, met0 = 2 * FIELDS, 2 * FIELDS + LEVELS
    loads = [pltpu.make_async_copy(ins[c], st.at[pl.ds(4 * c, 4), body], in_sem.at[c]) for c in range(4)]
    loads.append(pltpu.make_async_copy(ins[4], wet_i, in_sem.at[4]))
    loads.append(pltpu.make_async_copy(ins[5], floor_i, in_sem.at[5]))
    loads += [pltpu.make_async_copy(ins[6 + m], st.at[met0 + 1 + m, body], in_sem.at[6 + m]) for m in range(4)]
    loads.append(pltpu.make_async_copy(ins[10], st.at[pl.ds(met0 + 5, 3), body], in_sem.at[10]))
    for load in loads:
        load.start()

    e_lon, w_lon = lax.rem(lon + 1, nlon), lax.rem(lon + nlon - 1, nlon)
    n_lat = jnp.where(top, lat, lat + 1)
    n_lon = jnp.where(top, nlon - 1 - lon, lon)
    ne_lon = jnp.where(top, lax.rem(2 * nlon - 2 - lon, nlon), e_lon)
    nw_lon = jnp.where(top, lax.rem(nlon - lon, nlon), w_lon)
    s_lat = jnp.maximum(lat - 1, 0)
    ne_self = jnp.logical_and(top, ne_lon == lon)
    nw_self = jnp.logical_and(top, nw_lon == lon)
    ne_other = jnp.logical_not(ne_self)
    nw_other = jnp.logical_not(nw_self)
    inner = jnp.logical_not(bottom)

    @pl.when(bottom)
    def _():
        ext[0, 120:, :] = jnp.zeros((8, 128), f32)
        ext[1, 120:, :] = jnp.zeros((8, 128), f32)
        recv_r[1, : 2 * 5 * LEVELS, :] = jnp.zeros((2 * 5 * LEVELS, cols), f32)
        recv_r[1, 2 * 5 * LEVELS :, :] = jnp.ones((2 * ENTRIES - 10 * LEVELS, cols), f32)

    barrier = pltpu.get_barrier_semaphore()

    def greet(dev):
        pl.semaphore_signal(barrier, inc=1, device_id=dev, device_id_type=MESH)

    greet((e_lon, lat))
    greet((w_lon, lat))
    greet((n_lon, n_lat))

    @pl.when(ne_other)
    def _():
        greet((ne_lon, n_lat))

    @pl.when(nw_other)
    def _():
        greet((nw_lon, n_lat))

    @pl.when(inner)
    def _():
        greet((lon, s_lat))
        greet((e_lon, s_lat))
        greet((w_lon, s_lat))

    lane = lax.broadcasted_iota(jnp.int32, (8, 128), 1)
    sub = lax.broadcasted_iota(jnp.int32, (8, 128), 0)
    heights = [jnp.full((8, 128), h_ref[k], f32) for k in range(LEVELS)]
    inv_h2 = [1.0 / (h * h) for h in heights]

    for load in loads:
        load.wait()

    group = lane >> 2

    @pl.loop(0, chunks)
    def _(r):
        span = pl.ds(pl.multiple_of(8 * r, 8), 8)
        held = pl.ds(pl.multiple_of(PAD + 8 * r, 8), 8)
        packed = jnp.zeros((8, 128), f32)
        kept = []
        wet = [wet_i[k, span, :].astype(f32) for k in range(LEVELS)]
        for c in range(ENTRIES):
            ch, k = c // LEVELS, c % LEVELS
            at = c if ch < WET else c + FIELDS
            if ch < WET:
                val = st[at, held, :] * wet[k]
            elif ch == WET:
                val = wet[k]
            elif at == met0:
                val = floor_i[span, :].astype(f32)
            else:
                val = st[at, held, :]
            if at <= met0:
                kept.append((at, val))
            g = placed(c)
            packed = jnp.where(group == g, pltpu.roll(val, (4 * g + 2) % 128, 1), packed)
        pack[span, :] = packed
        for at, val in kept:
            st[at, held, :] = val

    def entries(load, save):
        @pl.loop(0, ENTRIES // 4)
        def _(g):
            at = 4 * g + FIELDS * (g >= FIELDS // 4).astype(jnp.int32)
            held = [load(4 * g + i, at + i) for i in range(4)]
            for i in range(4):
                save(4 * g + i, at + i, *held[i])

    def take_edges(c, at):
        return st[at, pl.ds(PAD, 2), :], st[at, pl.ds(PAD + rows - 2, 2), :]

    def put_edges(c, at, low, high):
        send_r[1, pl.ds(2 * c, 2), :] = low
        send_r[0, pl.ds(2 * c, 2), :] = high
        st[at, pl.ds(row0, 2), :] = high
        st[at, pl.ds(row0 + 6, 2), :] = low

    entries(take_edges, put_edges)

    @pl.when(top)
    def _():
        tiles = [send_r[0, pl.ds(8 * t, 8), :] for t in range(2 * ENTRIES // 8)]
        tiles = [jnp.where((sub & 1) == 1, pltpu.roll(v, 1, 0), pltpu.roll(v, 7, 0)) for v in tiles]
        step = 1
        while step < cols:
            far_half = (lane & step) != 0
            tiles = [jnp.where(far_half, pltpu.roll(v, step, 1), pltpu.roll(v, cols - step, 1)) for v in tiles]
            step *= 2
        for t, v in enumerate(tiles):
            send_r[0, pl.ds(8 * t, 8), :] = -v if 4 * LEVELS <= 8 * t < 8 * LEVELS else v

    last = pack[pl.ds(rows - 8, 8), :]
    turned = jnp.broadcast_to(last[7:8, :], (8, 128))
    for step in (1, 2):
        turned = jnp.where((lane & step) != 0, pltpu.roll(turned, step, 1), pltpu.roll(turned, 128 - step, 1))
    turned = jnp.where(jnp.logical_and(lane >= 8 * LEVELS, lane < 16 * LEVELS), -turned, turned)
    top_v = jnp.full((8, 128), topi) == 1
    folded = jnp.where(top_v, turned, last)
    corner[...] = folded

    @pl.when(ne_self)
    def _():
        ext[0, pl.ds(rows, 8), :] = folded

    @pl.when(nw_self)
    def _():
        ext[1, pl.ds(rows, 8), :] = folded

    pl.semaphore_wait(
        barrier,
        3 + ne_other.astype(jnp.int32) + nw_other.astype(jnp.int32) + 3 * inner.astype(jnp.int32),
    )

    def copy(src, dst, s, r, dev):
        return pltpu.make_async_remote_copy(
            src_ref=src, dst_ref=dst, send_sem=s_sem.at[s], recv_sem=r_sem.at[r], device_id=dev, device_id_type=MESH
        )

    whole, up, down = pl.ds(0, rows), pl.ds(rows, 8), pl.ds(120, 8)
    over = pl.ds(pl.multiple_of(120 - (120 - rows) * topi, 8), 8)
    to_east = copy(pack.at[whole], ext.at[1, whole], 0, 1, (e_lon, lat))
    to_west = copy(pack.at[whole], ext.at[0, whole], 1, 0, (w_lon, lat))
    to_n = copy(send_r.at[0], recv_r.at[1 - topi], 2, 3 - topi, (n_lon, n_lat))
    to_ne = copy(corner, ext.at[1 - topi, over], 4, 7 - 3 * topi, (ne_lon, n_lat))
    to_nw = copy(corner, ext.at[topi, over], 5, 6 - topi, (nw_lon, n_lat))
    to_s = copy(send_r.at[1], recv_r.at[0], 3, 2, (lon, s_lat))
    to_se = copy(pack.at[pl.ds(0, 8)], ext.at[1, up], 6, 5, (e_lon, s_lat))
    to_sw = copy(pack.at[pl.ds(0, 8)], ext.at[0, up], 7, 4, (w_lon, s_lat))
    from_s = copy(send_r.at[0], recv_r.at[1], 2, 3, (lon, s_lat))
    from_se = copy(corner, ext.at[0, down], 5, 6, (e_lon, s_lat))
    from_sw = copy(corner, ext.at[1, down], 4, 7, (w_lon, s_lat))

    to_n.start()
    to_east.start()
    to_west.start()

    @pl.when(ne_other)
    def _():
        to_ne.start()

    @pl.when(nw_other)
    def _():
        to_nw.start()

    @pl.when(inner)
    def _():
        to_s.start()
        to_se.start()
        to_sw.start()

    is_east = (lane & 3) == 2

    def arrive():
        to_s.wait_recv()

        @pl.when(inner)
        def _():
            from_s.wait_recv()
            from_se.wait_recv()
            from_sw.wait_recv()

        @pl.when(ne_other)
        def _():
            to_sw.wait_recv()

        @pl.when(nw_other)
        def _():
            to_se.wait_recv()

        to_west.wait_recv()
        to_east.wait_recv()

        pair = (lax.broadcasted_iota(jnp.int32, (128, 128), 1) >> 1) & 1

        @pl.loop(0, 2)
        def _(side):
            z[side] = jnp.transpose(jnp.where(pair != side, ext[side], pack[...]))

        def take_halo(c, at):
            two, four = pl.ds(2 * c, 2), pl.ds(4 * c, 4)
            return recv_r[0, two, :], recv_r[1, two, :], z[0, four, :], z[1, four, :]

        def put_halo(c, at, north, south, east, west):
            st[at, pl.ds(PAD + rows, 1), :] = north[0:1, :]
            st[at, pl.ds(PAD - 1, 1), :] = south[1:2, :]
            st[at, pl.ds(row0 + 2, 2), :] = north
            st[at, pl.ds(row0 + 4, 2), :] = south
            st[at, pl.ds(col0, 4), :] = east
            st[at, pl.ds(col0 + 4, 4), :] = west

        entries(take_halo, put_halo)
        st[met0 + 3, pl.ds(col0, 8), :] = -st[met0 + 3, pl.ds(col0, 8), :]

        @pl.loop(0, chunks)
        def _(r):
            span = pl.ds(pl.multiple_of(8 * r, 8), 8)
            hold[0, pl.ds(pl.multiple_of(PAD + 8 * r, 8), 8), :] = jnp.where(is_east, ext[0, span, :], ext[1, span, :])

        far_n = jnp.where(is_east, ext[0, up, :], ext[1, up, :])[0:1, :]
        far_s = jnp.where(is_east, ext[0, down, :], ext[1, down, :])[7:8, :]
        hold[0, pl.ds(row0, 8), :] = jnp.where(
            sub == 2, jnp.broadcast_to(far_n, (8, 128)), jnp.broadcast_to(far_s, (8, 128))
        )

    def between():
        @pl.loop(0, 5 * LEVELS // 4)
        def _(g):
            held = [(st[FIELDS + 4 * g + i, pl.ds(row0, 8), :], st[FIELDS + 4 * g + i, pl.ds(col0, 8), :]) for i in range(4)]
            for i, (about_row, about_col) in enumerate(held):
                c = 4 * g + i
                st[FIELDS + c, pl.ds(PAD + rows, 1), :] = about_row[2:3, :]
                st[FIELDS + c, pl.ds(PAD - 1, 1), :] = about_row[5:6, :]
                z[0, pl.ds(4 * c + 2, 1), :] = about_col[2:3, :]
                z[0, pl.ds(4 * c + 1, 1), :] = about_col[5:6, :]
                z[1, pl.ds(4 * c + 2, 1), :] = about_col[6:7, :]
                z[1, pl.ds(4 * c + 1, 1), :] = about_col[1:2, :]

        hold[1, body, :] = jnp.transpose(z[0])[:rows, :]
        hold[0, body, :] = jnp.transpose(z[1])[:rows, :]

        @pl.loop(1, chunks - 1)
        def _(r):
            held = pl.ds(pl.multiple_of(PAD + 8 * r, 8), 8)
            own = hold[0, held, :]
            outer = jnp.logical_or(lane == 0, lane == 127)
            vals = [st[FIELDS + c, held, :] for c in range(FIELDS)]
            for c in range(FIELDS):
                ends = pltpu.roll(own, (126 - 4 * placed(c)) % 128, 1)
                st[FIELDS + c, held, :] = jnp.where(outer, ends, vals[c])

    ahead = (chunks - 2) // 2
    flag = lambda cond: cond.astype(jnp.int32)

    def tile_values(p, i):
        second = flag(p >= ahead + 2)
        early = flag(p < ahead)
        outer = flag(p == ahead)
        slabs = flag(p == ahead + 1)
        tile = (
            early * (1 + 2 * p + i) + outer * (i * (chunks - 1)) + slabs * (chunks + i)
            + second * (2 * (p - ahead - 2) + i)
        )
        off = pl.multiple_of(PAD + 8 * (tile + slabs), 8)
        held = pl.ds(off, 8)
        src = FIELDS * second
        dst = FIELDS - src
        turned_tile = early + slabs * i
        at_first = lane == 0 - turned_tile
        at_last = lane == 127 + turned_tile
        ends_all = hold[second, held, :]

        def side_of(c, val):
            ends = pltpu.roll(ends_all, (126 - 4 * placed(c)) % 128, 1)
            east = pltpu.roll(jnp.where(at_first, ends, val), 127, 1)
            west = pltpu.roll(jnp.where(at_last, ends, val), 1, 1)
            return east, west

        def around(c, at):
            val = st[at, held, :]
            return (val, *side_of(c, val), st[at, pl.ds(off + 1, 8), :], st[at, pl.ds(off - 1, 8), :])

        floor, zs, ms, rot, eddy, *mix = [st[met0 + m, held, :] for m in range(8)]
        rz, rm = 1.0 / zs, 1.0 / ms
        kx, ky, hx, hy = eddy * rz * rz, eddy * rm * rm, 0.5 * rz, 0.5 * rm
        results = []
        sum_x = sum_y = None
        for k in range(LEVELS):
            wet, we, ww, wn, ws = around(WET * LEVELS + k, wet0 + k)
            dtw = TIME_STEP * wet
            ax, ay = dtw * kx, dtw * ky
            bx, by, br = dtw * hx, dtw * hy, dtw * rot
            ae, aw, an, as_ = ax * we, ax * ww, ay * wn, ay * ws
            centre = 1.0 - (ae + aw) - (an + as_)
            t2 = dtw * inv_h2[k]
            below = above = None
            if k < LEVELS - 1:
                below = t2 * mix[k] * st[wet0 + k + 1, held, :]
                centre = centre - below
            if k > 0:
                above = t2 * mix[k - 1] * st[wet0 + k - 1, held, :]
                centre = centre - above
            drag = centre - jnp.where(floor == float(k), BOTTOM_DRAG * dtw, 0.0)
            u, v = st[src + 2 * LEVELS + k, held, :], st[src + 3 * LEVELS + k, held, :]
            bu, bv = bx * u, by * v
            ce, cw, cn, cs = ae - bu, aw + bu, an - bv, as_ + bv
            layer_x = layer_y = None
            for ch in range(4):
                c = ch * LEVELS + k
                val, east, west, north, south = around(c, src + c)
                new = (centre if ch < 2 else drag) * val + (ce * east + cw * west) + (cn * north + cs * south)
                if below is not None:
                    new = new + below * st[src + c + 1, held, :]
                if above is not None:
                    new = new + above * st[src + c - 1, held, :]
                if ch == 0:
                    layer_x, layer_y = EXPANSION * (west - east), EXPANSION * (south - north)
                if ch == 1:
                    layer_x = (layer_x + CONTRACTION * (east - west)) * heights[k]
                    layer_y = (layer_y + CONTRACTION * (north - south)) * heights[k]
                    sum_x = layer_x if k == 0 else sum_x + layer_x
                    sum_y = layer_y if k == 0 else sum_y + layer_y
                if ch == 2:
                    new = new + br * v - bx * (sum_x - 0.5 * layer_x)
                if ch == 3:
                    new = new - br * u - by * (sum_y - 0.5 * layer_y)
                results.append((c, new))
        return dst, held, results

    @pl.loop(0, ahead + 2 + chunks // 2)
    def _(p):
        pl.when(p == ahead)(arrive)
        pl.when(p == ahead + 2)(between)
        done = [tile_values(p, i) for i in range(2)]
        for dst, held, results in done:
            for c, new in results:
                st[dst + c, held, :] = new

    stores = [pltpu.make_async_copy(st.at[pl.ds(4 * c, 4), body], outs[c], out_sem.at[c]) for c in range(4)]
    for store in stores:
        store.start()

    to_east.wait_send()
    to_west.wait_send()
    to_n.wait_send()

    @pl.when(ne_other)
    def _():
        to_ne.wait_send()

    @pl.when(nw_other)
    def _():
        to_nw.wait_send()

    @pl.when(inner)
    def _():
        to_s.wait_send()
        to_se.wait_send()
        to_sw.wait_send()

    for store in stores:
        store.wait()


def hand_over(*refs):
    held, sem_in, sem_out = refs[8:]
    moves = [pltpu.make_async_copy(refs[c], held.at[c], sem_in.at[c]) for c in range(4)]
    stores = [pltpu.make_async_copy(held.at[c], refs[4 + c], sem_out.at[c]) for c in range(4)]
    for move in moves:
        move.start()
    for move, store in zip(moves, stores):
        move.wait()
        store.start()
    for store in stores:
        store.wait()


def solution(mesh):
    nlon, nlat = mesh.shape["lon"], mesh.shape["lat"]

    def shards(*args):
        levels, rows, cols = args[0].shape
        f32 = jnp.float32
        vmem = pltpu.VMEM
        held = rows + 5 * PAD
        hbm = pl.BlockSpec(memory_space=pltpu.HBM)
        out_shape = [jax.ShapeDtypeStruct((levels, rows, cols), f32)] * 4
        results = pl.pallas_call(
            functools.partial(kernel, nlon, nlat, rows, cols),
            out_shape=out_shape,
            in_specs=[hbm] * 11 + [pl.BlockSpec(memory_space=pltpu.SMEM)],
            out_specs=[hbm] * 4,
            scratch_shapes=[
                vmem((2 * FIELDS + ENTRIES - FIELDS, held, cols), f32),
                vmem((2, held, 128), f32),
                vmem((levels, rows, cols), jnp.int32),
                vmem((rows, cols), jnp.int32),
                vmem((128, 128), f32),
                vmem((2, 128, 128), f32),
                vmem((2, 2 * ENTRIES, cols), f32),
                vmem((2, 2 * ENTRIES, cols), f32),
                vmem((8, 128), f32),
                vmem((2, 128, 128), f32),
                pltpu.SemaphoreType.DMA((11,)),
                pltpu.SemaphoreType.DMA((4,)),
                pltpu.SemaphoreType.DMA((8,)),
                pltpu.SemaphoreType.DMA((8,)),
            ],
            compiler_params=pltpu.CompilerParams(
                collective_id=0, has_side_effects=True, vmem_limit_bytes=60 * 1024 * 1024
            ),
        )(*args)
        return tuple(pl.pallas_call(
            hand_over,
            out_shape=out_shape,
            in_specs=[hbm] * 4,
            out_specs=[hbm] * 4,
            scratch_shapes=[vmem((4, levels, rows, cols), f32), pltpu.SemaphoreType.DMA((4,)), pltpu.SemaphoreType.DMA((4,))],
            compiler_params=pltpu.CompilerParams(vmem_limit_bytes=60 * 1024 * 1024),
        )(*results))

    field, plane = P(None, "lat", "lon"), P("lat", "lon")
    return jax.shard_map(
        shards,
        mesh=mesh,
        in_specs=(field,) * 5 + (plane,) * 5 + (field, P()),
        out_specs=(field,) * 4,
        check_vma=False,
    )
```

```python
import functools

import jax
import jax.numpy as jnp
from jax import lax
from jax.experimental import pallas as pl
from jax.experimental.pallas import tpu as pltpu
from jax.sharding import PartitionSpec as P

MESH = pl.DeviceIdType.MESH
TIME_STEP = 0.25
EXPANSION = 0.2
CONTRACTION = 0.8
BOTTOM_DRAG = 1.0
LEVELS = 4
ENTRIES = 28
FIELDS = 16
WET = 4
PAD = 8


def placed(c):
    if 8 <= c < 12:
        return c + 4
    if 12 <= c < 16:
        return c - 4
    return {21: 22, 22: 21}.get(c, c)


def kernel(nlon, nlat, rows, cols, *refs):
    ins, h_ref = refs[:11], refs[11]
    outs = refs[12:16]
    (st, hold, wet_i, floor_i, pack, ext, send_r, recv_r, corner, z, in_sem, s_sem, r_sem) = refs[16:]
    lon, lat = lax.axis_index("lon"), lax.axis_index("lat")
    top, bottom = lat == nlat - 1, lat == 0
    topi = top.astype(jnp.int32)
    f32 = jnp.float32
    chunks = rows // 8
    row_tile, col_tile = chunks, chunks + 1
    row0, col0 = PAD + 8 * (chunks + 1), PAD + 8 * (chunks + 2)
    body = pl.ds(PAD, rows)

    wet0, met0 = 2 * FIELDS, 2 * FIELDS + LEVELS
    loads = [pltpu.make_async_copy(ins[c], st.at[pl.ds(4 * c, 4), body], in_sem.at[c]) for c in range(4)]
    loads.append(pltpu.make_async_copy(ins[4], wet_i, in_sem.at[4]))
    loads.append(pltpu.make_async_copy(ins[5], floor_i, in_sem.at[5]))
    loads += [pltpu.make_async_copy(ins[6 + m], st.at[met0 + 1 + m, body], in_sem.at[6 + m]) for m in range(4)]
    loads.append(pltpu.make_async_copy(ins[10], st.at[pl.ds(met0 + 5, 3), body], in_sem.at[10]))
    for load in loads:
        load.start()

    e_lon, w_lon = lax.rem(lon + 1, nlon), lax.rem(lon + nlon - 1, nlon)
    n_lat = jnp.where(top, lat, lat + 1)
    n_lon = jnp.where(top, nlon - 1 - lon, lon)
    ne_lon = jnp.where(top, lax.rem(2 * nlon - 2 - lon, nlon), e_lon)
    nw_lon = jnp.where(top, lax.rem(nlon - lon, nlon), w_lon)
    s_lat = jnp.maximum(lat - 1, 0)
    ne_self = jnp.logical_and(top, ne_lon == lon)
    nw_self = jnp.logical_and(top, nw_lon == lon)
    ne_other = jnp.logical_not(ne_self)
    nw_other = jnp.logical_not(nw_self)
    inner = jnp.logical_not(bottom)

    @pl.when(bottom)
    def _():
        ext[0, 120:, :] = jnp.zeros((8, 128), f32)
        ext[1, 120:, :] = jnp.zeros((8, 128), f32)
        recv_r[1, : 2 * 5 * LEVELS, :] = jnp.zeros((2 * 5 * LEVELS, cols), f32)
        recv_r[1, 2 * 5 * LEVELS :, :] = jnp.ones((2 * ENTRIES - 10 * LEVELS, cols), f32)

    barrier = pltpu.get_barrier_semaphore()

    def greet(dev):
        pl.semaphore_signal(barrier, inc=1, device_id=dev, device_id_type=MESH)

    greet((e_lon, lat))
    greet((w_lon, lat))
    greet((n_lon, n_lat))

    @pl.when(ne_other)
    def _():
        greet((ne_lon, n_lat))

    @pl.when(nw_other)
    def _():
        greet((nw_lon, n_lat))

    @pl.when(inner)
    def _():
        greet((lon, s_lat))
        greet((e_lon, s_lat))
        greet((w_lon, s_lat))

    lane = lax.broadcasted_iota(jnp.int32, (8, 128), 1)
    sub = lax.broadcasted_iota(jnp.int32, (8, 128), 0)
    heights = [jnp.full((8, 128), h_ref[k], f32) for k in range(LEVELS)]
    inv_h2 = [1.0 / (h * h) for h in heights]

    for load in loads:
        load.wait()

    group = lane >> 2

    def masked(r):
        span = pl.ds(pl.multiple_of(8 * r, 8), 8)
        held = pl.ds(pl.multiple_of(PAD + 8 * r, 8), 8)
        packed = jnp.zeros((8, 128), f32)
        kept = []
        wet = [wet_i[k, span, :].astype(f32) for k in range(LEVELS)]
        for c in range(ENTRIES):
            ch, k = c // LEVELS, c % LEVELS
            at = c if ch < WET else c + FIELDS
            if ch < WET:
                val = st[at, held, :] * wet[k]
            elif ch == WET:
                val = wet[k]
            elif at == met0:
                val = floor_i[span, :].astype(f32)
            else:
                val = st[at, held, :]
            if at <= met0:
                kept.append((at, val))
            g = placed(c)
            packed = jnp.where(group == g, pltpu.roll(val, (4 * g + 2) % 128, 1), packed)
        return span, held, packed, kept

    @pl.loop(0, chunks // 2)
    def _(r):
        for span, held, packed, kept in [masked(2 * r + i) for i in range(2)]:
            pack[span, :] = packed
            for at, val in kept:
                st[at, held, :] = val

    def entries(load, save):
        @pl.loop(0, ENTRIES // 4)
        def _(g):
            at = 4 * g + FIELDS * (g >= FIELDS // 4).astype(jnp.int32)
            held = [load(4 * g + i, at + i) for i in range(4)]
            for i in range(4):
                save(4 * g + i, at + i, *held[i])

    def take_edges(c, at):
        return st[at, pl.ds(PAD, 2), :], st[at, pl.ds(PAD + rows - 2, 2), :]

    def put_edges(c, at, low, high):
        send_r[1, pl.ds(2 * c, 2), :] = low
        send_r[0, pl.ds(2 * c, 2), :] = high
        st[at, pl.ds(row0, 2), :] = high
        st[at, pl.ds(row0 + 6, 2), :] = low

    entries(take_edges, put_edges)

    @pl.when(top)
    def _():
        tiles = [send_r[0, pl.ds(8 * t, 8), :] for t in range(2 * ENTRIES // 8)]
        tiles = [jnp.where((sub & 1) == 1, pltpu.roll(v, 1, 0), pltpu.roll(v, 7, 0)) for v in tiles]
        step = 1
        while step < cols:
            far_half = (lane & step) != 0
            tiles = [jnp.where(far_half, pltpu.roll(v, step, 1), pltpu.roll(v, cols - step, 1)) for v in tiles]
            step *= 2
        for t, v in enumerate(tiles):
            send_r[0, pl.ds(8 * t, 8), :] = -v if 4 * LEVELS <= 8 * t < 8 * LEVELS else v

    last = pack[pl.ds(rows - 8, 8), :]
    turned = jnp.broadcast_to(last[7:8, :], (8, 128))
    for step in (1, 2):
        turned = jnp.where((lane & step) != 0, pltpu.roll(turned, step, 1), pltpu.roll(turned, 128 - step, 1))
    turned = jnp.where(jnp.logical_and(lane >= 8 * LEVELS, lane < 16 * LEVELS), -turned, turned)
    top_v = jnp.full((8, 128), topi) == 1
    folded = jnp.where(top_v, turned, last)
    corner[...] = folded

    @pl.when(ne_self)
    def _():
        ext[0, pl.ds(rows, 8), :] = folded

    @pl.when(nw_self)
    def _():
        ext[1, pl.ds(rows, 8), :] = folded

    pl.semaphore_wait(
        barrier,
        3 + ne_other.astype(jnp.int32) + nw_other.astype(jnp.int32) + 3 * inner.astype(jnp.int32),
    )

    def copy(src, dst, s, r, dev):
        return pltpu.make_async_remote_copy(
            src_ref=src, dst_ref=dst, send_sem=s_sem.at[s], recv_sem=r_sem.at[r], device_id=dev, device_id_type=MESH
        )

    whole, up, down = pl.ds(0, rows), pl.ds(rows, 8), pl.ds(120, 8)
    over = pl.ds(pl.multiple_of(120 - (120 - rows) * topi, 8), 8)
    to_east = copy(pack.at[whole], ext.at[1, whole], 0, 1, (e_lon, lat))
    to_west = copy(pack.at[whole], ext.at[0, whole], 1, 0, (w_lon, lat))
    to_n = copy(send_r.at[0], recv_r.at[1 - topi], 2, 3 - topi, (n_lon, n_lat))
    to_ne = copy(corner, ext.at[1 - topi, over], 4, 7 - 3 * topi, (ne_lon, n_lat))
    to_nw = copy(corner, ext.at[topi, over], 5, 6 - topi, (nw_lon, n_lat))
    to_s = copy(send_r.at[1], recv_r.at[0], 3, 2, (lon, s_lat))
    to_se = copy(pack.at[pl.ds(0, 8)], ext.at[1, up], 6, 5, (e_lon, s_lat))
    to_sw = copy(pack.at[pl.ds(0, 8)], ext.at[0, up], 7, 4, (w_lon, s_lat))
    from_s = copy(send_r.at[0], recv_r.at[1], 2, 3, (lon, s_lat))
    from_se = copy(corner, ext.at[0, down], 5, 6, (e_lon, s_lat))
    from_sw = copy(corner, ext.at[1, down], 4, 7, (w_lon, s_lat))

    to_n.start()
    to_east.start()
    to_west.start()

    @pl.when(ne_other)
    def _():
        to_ne.start()

    @pl.when(nw_other)
    def _():
        to_nw.start()

    @pl.when(inner)
    def _():
        to_s.start()
        to_se.start()
        to_sw.start()

    is_east = (lane & 3) == 2

    def arrive():
        to_s.wait_recv()

        @pl.when(inner)
        def _():
            from_s.wait_recv()
            from_se.wait_recv()
            from_sw.wait_recv()

        @pl.when(ne_other)
        def _():
            to_sw.wait_recv()

        @pl.when(nw_other)
        def _():
            to_se.wait_recv()

        to_west.wait_recv()
        to_east.wait_recv()

        pair = (lax.broadcasted_iota(jnp.int32, (128, 128), 1) >> 1) & 1

        @pl.loop(0, 2)
        def _(side):
            z[side] = jnp.transpose(jnp.where(pair != side, ext[side], pack[...]))

        def take_halo(c, at):
            two, four = pl.ds(2 * c, 2), pl.ds(4 * c, 4)
            return recv_r[0, two, :], recv_r[1, two, :], z[0, four, :], z[1, four, :]

        def put_halo(c, at, north, south, east, west):
            st[at, pl.ds(PAD + rows, 1), :] = north[0:1, :]
            st[at, pl.ds(PAD - 1, 1), :] = south[1:2, :]
            st[at, pl.ds(row0 + 2, 2), :] = north
            st[at, pl.ds(row0 + 4, 2), :] = south
            st[at, pl.ds(col0, 4), :] = east
            st[at, pl.ds(col0 + 4, 4), :] = west

        entries(take_halo, put_halo)
        st[met0 + 3, pl.ds(col0, 8), :] = -st[met0 + 3, pl.ds(col0, 8), :]

        @pl.loop(0, chunks)
        def _(r):
            span = pl.ds(pl.multiple_of(8 * r, 8), 8)
            hold[0, pl.ds(pl.multiple_of(PAD + 8 * r, 8), 8), :] = jnp.where(is_east, ext[0, span, :], ext[1, span, :])

        far_n = jnp.where(is_east, ext[0, up, :], ext[1, up, :])[0:1, :]
        far_s = jnp.where(is_east, ext[0, down, :], ext[1, down, :])[7:8, :]
        hold[0, pl.ds(row0, 8), :] = jnp.where(
            sub == 2, jnp.broadcast_to(far_n, (8, 128)), jnp.broadcast_to(far_s, (8, 128))
        )

    def between():
        @pl.loop(0, 5 * LEVELS // 4)
        def _(g):
            held = [(st[FIELDS + 4 * g + i, pl.ds(row0, 8), :], st[FIELDS + 4 * g + i, pl.ds(col0, 8), :]) for i in range(4)]
            for i, (about_row, about_col) in enumerate(held):
                c = 4 * g + i
                st[FIELDS + c, pl.ds(PAD + rows, 1), :] = about_row[2:3, :]
                st[FIELDS + c, pl.ds(PAD - 1, 1), :] = about_row[5:6, :]
                z[0, pl.ds(4 * c + 2, 1), :] = about_col[2:3, :]
                z[0, pl.ds(4 * c + 1, 1), :] = about_col[5:6, :]
                z[1, pl.ds(4 * c + 2, 1), :] = about_col[6:7, :]
                z[1, pl.ds(4 * c + 1, 1), :] = about_col[1:2, :]

        hold[1, body, :] = jnp.transpose(z[0])[:rows, :]
        hold[0, body, :] = jnp.transpose(z[1])[:rows, :]

        @pl.loop(0, (chunks - 2) // 2)
        def _(r):
            outer = jnp.logical_or(lane == 0, lane == 127)
            patched = []
            for i in range(2):
                held = pl.ds(pl.multiple_of(PAD + 8 * (1 + 2 * r + i), 8), 8)
                own = hold[0, held, :]
                for c in range(FIELDS):
                    ends = pltpu.roll(own, (126 - 4 * placed(c)) % 128, 1)
                    patched.append((c, held, jnp.where(outer, ends, st[FIELDS + c, held, :])))
            for c, held, val in patched:
                st[FIELDS + c, held, :] = val

    ahead = (chunks - 2) // 2
    flag = lambda cond: cond.astype(jnp.int32)

    def tile_values(p, i):
        second = flag(p >= ahead + 2)
        early = flag(p < ahead)
        outer = flag(p == ahead)
        slabs = flag(p == ahead + 1)
        tile = (
            early * (1 + 2 * p + i) + outer * (i * (chunks - 1)) + slabs * (chunks + i)
            + second * (2 * (p - ahead - 2) + i)
        )
        off = pl.multiple_of(PAD + 8 * (tile + slabs), 8)
        held = pl.ds(off, 8)
        src = FIELDS * second
        dst = FIELDS - src
        turned_tile = early + slabs * i
        at_first = lane == 0 - turned_tile
        at_last = lane == 127 + turned_tile
        ends_all = hold[second, held, :]

        def side_of(c, val):
            ends = pltpu.roll(ends_all, (126 - 4 * placed(c)) % 128, 1)
            east = pltpu.roll(jnp.where(at_first, ends, val), 127, 1)
            west = pltpu.roll(jnp.where(at_last, ends, val), 1, 1)
            return east, west

        def around(c, at):
            val = st[at, held, :]
            return (val, *side_of(c, val), st[at, pl.ds(off + 1, 8), :], st[at, pl.ds(off - 1, 8), :])

        floor, zs, ms, rot, eddy, *mix = [st[met0 + m, held, :] for m in range(8)]
        rz, rm = 1.0 / zs, 1.0 / ms
        kx, ky, hx, hy = eddy * rz * rz, eddy * rm * rm, 0.5 * rz, 0.5 * rm
        results = []
        sum_x = sum_y = None
        for k in range(LEVELS):
            wet, we, ww, wn, ws = around(WET * LEVELS + k, wet0 + k)
            dtw = TIME_STEP * wet
            ax, ay = dtw * kx, dtw * ky
            bx, by, br = dtw * hx, dtw * hy, dtw * rot
            ae, aw, an, as_ = ax * we, ax * ww, ay * wn, ay * ws
            centre = 1.0 - (ae + aw) - (an + as_)
            t2 = dtw * inv_h2[k]
            below = above = None
            if k < LEVELS - 1:
                below = t2 * mix[k] * st[wet0 + k + 1, held, :]
                centre = centre - below
            if k > 0:
                above = t2 * mix[k - 1] * st[wet0 + k - 1, held, :]
                centre = centre - above
            drag = centre - jnp.where(floor == float(k), BOTTOM_DRAG * dtw, 0.0)
            u, v = st[src + 2 * LEVELS + k, held, :], st[src + 3 * LEVELS + k, held, :]
            bu, bv = bx * u, by * v
            ce, cw, cn, cs = ae - bu, aw + bu, an - bv, as_ + bv
            layer_x = layer_y = None
            for ch in range(4):
                c = ch * LEVELS + k
                val, east, west, north, south = around(c, src + c)
                new = (centre if ch < 2 else drag) * val + (ce * east + cw * west) + (cn * north + cs * south)
                if below is not None:
                    new = new + below * st[src + c + 1, held, :]
                if above is not None:
                    new = new + above * st[src + c - 1, held, :]
                if ch == 0:
                    layer_x, layer_y = EXPANSION * (west - east), EXPANSION * (south - north)
                if ch == 1:
                    layer_x = (layer_x + CONTRACTION * (east - west)) * heights[k]
                    layer_y = (layer_y + CONTRACTION * (north - south)) * heights[k]
                    sum_x = layer_x if k == 0 else sum_x + layer_x
                    sum_y = layer_y if k == 0 else sum_y + layer_y
                if ch == 2:
                    new = new + br * v - bx * (sum_x - 0.5 * layer_x)
                if ch == 3:
                    new = new - br * u - by * (sum_y - 0.5 * layer_y)
                results.append((c, new))
        return dst, held, results

    @pl.loop(0, ahead + 2 + chunks // 2)
    def _(p):
        pl.when(p == ahead)(arrive)
        pl.when(p == ahead + 2)(between)
        done = [tile_values(p, i) for i in range(2)]
        for dst, held, results in done:
            for c, new in results:
                st[dst + c, held, :] = new

    @pl.loop(0, chunks)
    def _(r):
        held = pl.ds(pl.multiple_of(PAD + 8 * r, 8), 8)
        vals = [st[c, held, :] for c in range(FIELDS)]
        for c in range(FIELDS):
            outs[c // LEVELS][c % LEVELS, pl.ds(pl.multiple_of(8 * r, 8), 8), :] = vals[c]

    to_east.wait_send()
    to_west.wait_send()
    to_n.wait_send()

    @pl.when(ne_other)
    def _():
        to_ne.wait_send()

    @pl.when(nw_other)
    def _():
        to_nw.wait_send()

    @pl.when(inner)
    def _():
        to_s.wait_send()
        to_se.wait_send()
        to_sw.wait_send()


def hand_over(*refs):
    moves = [pltpu.make_async_copy(refs[c], refs[4 + c], refs[8].at[c]) for c in range(4)]
    for move in moves:
        move.start()
    for move in moves:
        move.wait()


def solution(mesh):
    nlon, nlat = mesh.shape["lon"], mesh.shape["lat"]

    def shards(*args):
        levels, rows, cols = args[0].shape
        f32 = jnp.float32
        vmem = pltpu.VMEM
        held = rows + 5 * PAD
        hbm = pl.BlockSpec(memory_space=pltpu.HBM)
        out_shape = [jax.ShapeDtypeStruct((levels, rows, cols), f32)] * 4
        results = pl.pallas_call(
            functools.partial(kernel, nlon, nlat, rows, cols),
            out_shape=[pltpu.VMEM((levels, rows, cols), f32)] * 4,
            in_specs=[hbm] * 11 + [pl.BlockSpec(memory_space=pltpu.SMEM)],
            out_specs=[pl.BlockSpec(memory_space=pltpu.VMEM)] * 4,
            scratch_shapes=[
                vmem((2 * FIELDS + ENTRIES - FIELDS, held, cols), f32),
                vmem((2, held, 128), f32),
                vmem((levels, rows, cols), jnp.int32),
                vmem((rows, cols), jnp.int32),
                vmem((128, 128), f32),
                vmem((2, 128, 128), f32),
                vmem((2, 2 * ENTRIES, cols), f32),
                vmem((2, 2 * ENTRIES, cols), f32),
                vmem((8, 128), f32),
                vmem((2, 128, 128), f32),
                pltpu.SemaphoreType.DMA((11,)),
                pltpu.SemaphoreType.DMA((8,)),
                pltpu.SemaphoreType.DMA((8,)),
            ],
            compiler_params=pltpu.CompilerParams(
                collective_id=0, has_side_effects=True, vmem_limit_bytes=60 * 1024 * 1024
            ),
        )(*args)
        return tuple(pl.pallas_call(
            hand_over,
            out_shape=out_shape,
            in_specs=[pl.BlockSpec(memory_space=pltpu.VMEM)] * 4,
            out_specs=[hbm] * 4,
            scratch_shapes=[pltpu.SemaphoreType.DMA((4,))],
            compiler_params=pltpu.CompilerParams(vmem_limit_bytes=16 * 1024 * 1024),
        )(*results))

    field, plane = P(None, "lat", "lon"), P("lat", "lon")
    return jax.shard_map(
        shards,
        mesh=mesh,
        in_specs=(field,) * 5 + (plane,) * 5 + (field, P()),
        out_specs=(field,) * 4,
        check_vma=False,
    )
```

```python
import functools

import jax
import jax.numpy as jnp
from jax import lax
from jax.experimental import pallas as pl
from jax.experimental.pallas import tpu as pltpu
from jax.sharding import PartitionSpec as P

MESH = pl.DeviceIdType.MESH
TIME_STEP = 0.25
EXPANSION = 0.2
CONTRACTION = 0.8
BOTTOM_DRAG = 1.0
LEVELS = 4
ENTRIES = 28
FIELDS = 16
WET = 4
PAD = 8


def placed(c):
    if 8 <= c < 12:
        return c + 4
    if 12 <= c < 16:
        return c - 4
    return {21: 22, 22: 21}.get(c, c)


def kernel(nlon, nlat, rows, cols, *refs):
    ins, h_ref = refs[:11], refs[11]
    outs = refs[12:16]
    (st, hold, wet_i, floor_i, pack, ext, send_r, recv_r, corner, z, in_sem, s_sem, r_sem) = refs[16:]
    lon, lat = lax.axis_index("lon"), lax.axis_index("lat")
    top, bottom = lat == nlat - 1, lat == 0
    topi = top.astype(jnp.int32)
    f32 = jnp.float32
    chunks = rows // 8
    row_tile, col_tile = chunks, chunks + 1
    row0, col0 = PAD + 8 * (chunks + 1), PAD + 8 * (chunks + 2)
    body = pl.ds(PAD, rows)

    wet0, met0 = 2 * FIELDS, 2 * FIELDS + LEVELS
    loads = [pltpu.make_async_copy(ins[c], st.at[pl.ds(4 * c, 4), body], in_sem.at[c]) for c in range(4)]
    loads.append(pltpu.make_async_copy(ins[4], wet_i, in_sem.at[4]))
    loads.append(pltpu.make_async_copy(ins[5], floor_i, in_sem.at[5]))
    loads += [pltpu.make_async_copy(ins[6 + m], st.at[met0 + 1 + m, body], in_sem.at[6 + m]) for m in range(4)]
    loads.append(pltpu.make_async_copy(ins[10], st.at[pl.ds(met0 + 5, 3), body], in_sem.at[10]))
    for load in loads:
        load.start()

    e_lon, w_lon = lax.rem(lon + 1, nlon), lax.rem(lon + nlon - 1, nlon)
    n_lat = jnp.where(top, lat, lat + 1)
    n_lon = jnp.where(top, nlon - 1 - lon, lon)
    ne_lon = jnp.where(top, lax.rem(2 * nlon - 2 - lon, nlon), e_lon)
    nw_lon = jnp.where(top, lax.rem(nlon - lon, nlon), w_lon)
    s_lat = jnp.maximum(lat - 1, 0)
    ne_self = jnp.logical_and(top, ne_lon == lon)
    nw_self = jnp.logical_and(top, nw_lon == lon)
    ne_other = jnp.logical_not(ne_self)
    nw_other = jnp.logical_not(nw_self)
    inner = jnp.logical_not(bottom)

    @pl.when(bottom)
    def _():
        ext[0, 120:, :] = jnp.zeros((8, 128), f32)
        ext[1, 120:, :] = jnp.zeros((8, 128), f32)
        recv_r[1, : 2 * 5 * LEVELS, :] = jnp.zeros((2 * 5 * LEVELS, cols), f32)
        recv_r[1, 2 * 5 * LEVELS :, :] = jnp.ones((2 * ENTRIES - 10 * LEVELS, cols), f32)

    barrier = pltpu.get_barrier_semaphore()

    def greet(dev):
        pl.semaphore_signal(barrier, inc=1, device_id=dev, device_id_type=MESH)

    greet((e_lon, lat))
    greet((w_lon, lat))
    greet((n_lon, n_lat))

    @pl.when(ne_other)
    def _():
        greet((ne_lon, n_lat))

    @pl.when(nw_other)
    def _():
        greet((nw_lon, n_lat))

    @pl.when(inner)
    def _():
        greet((lon, s_lat))
        greet((e_lon, s_lat))
        greet((w_lon, s_lat))

    lane = lax.broadcasted_iota(jnp.int32, (8, 128), 1)
    sub = lax.broadcasted_iota(jnp.int32, (8, 128), 0)
    heights = [jnp.full((8, 128), h_ref[k], f32) for k in range(LEVELS)]
    inv_h2 = [1.0 / (h * h) for h in heights]

    for load in loads:
        load.wait()

    group = lane >> 2

    def masked(r):
        span = pl.ds(pl.multiple_of(8 * r, 8), 8)
        held = pl.ds(pl.multiple_of(PAD + 8 * r, 8), 8)
        packed = jnp.zeros((8, 128), f32)
        kept = []
        wet = [wet_i[k, span, :].astype(f32) for k in range(LEVELS)]
        for c in range(ENTRIES):
            ch, k = c // LEVELS, c % LEVELS
            at = c if ch < WET else c + FIELDS
            if ch < WET:
                val = st[at, held, :] * wet[k]
            elif ch == WET:
                val = wet[k]
            elif at == met0:
                val = floor_i[span, :].astype(f32)
            else:
                val = st[at, held, :]
            if at <= met0:
                kept.append((at, val))
            g = placed(c)
            packed = jnp.where(group == g, pltpu.roll(val, (4 * g + 2) % 128, 1), packed)
        return span, held, packed, kept

    @pl.loop(0, chunks // 2)
    def _(r):
        for span, held, packed, kept in [masked(2 * r + i) for i in range(2)]:
            pack[span, :] = packed
            for at, val in kept:
                st[at, held, :] = val

    def entries(load, save):
        @pl.loop(0, ENTRIES // 4)
        def _(g):
            at = 4 * g + FIELDS * (g >= FIELDS // 4).astype(jnp.int32)
            held = [load(4 * g + i, at + i) for i in range(4)]
            for i in range(4):
                save(4 * g + i, at + i, *held[i])

    last = pack[pl.ds(rows - 8, 8), :]
    turned = jnp.broadcast_to(last[7:8, :], (8, 128))
    for step in (1, 2):
        turned = jnp.where((lane & step) != 0, pltpu.roll(turned, step, 1), pltpu.roll(turned, 128 - step, 1))
    turned = jnp.where(jnp.logical_and(lane >= 8 * LEVELS, lane < 16 * LEVELS), -turned, turned)
    top_v = jnp.full((8, 128), topi) == 1
    folded = jnp.where(top_v, turned, last)
    corner[...] = folded

    @pl.when(ne_self)
    def _():
        ext[0, pl.ds(rows, 8), :] = folded

    @pl.when(nw_self)
    def _():
        ext[1, pl.ds(rows, 8), :] = folded

    pl.semaphore_wait(
        barrier,
        3 + ne_other.astype(jnp.int32) + nw_other.astype(jnp.int32) + 3 * inner.astype(jnp.int32),
    )

    def copy(src, dst, s, r, dev):
        return pltpu.make_async_remote_copy(
            src_ref=src, dst_ref=dst, send_sem=s_sem.at[s], recv_sem=r_sem.at[r], device_id=dev, device_id_type=MESH
        )

    whole, up, down = pl.ds(0, rows), pl.ds(rows, 8), pl.ds(120, 8)
    over = pl.ds(pl.multiple_of(120 - (120 - rows) * topi, 8), 8)
    to_east = copy(pack.at[whole], ext.at[1, whole], 0, 1, (e_lon, lat))
    to_west = copy(pack.at[whole], ext.at[0, whole], 1, 0, (w_lon, lat))
    to_n = copy(send_r.at[0], recv_r.at[1 - topi], 2, 3 - topi, (n_lon, n_lat))
    to_ne = copy(corner, ext.at[1 - topi, over], 4, 7 - 3 * topi, (ne_lon, n_lat))
    to_nw = copy(corner, ext.at[topi, over], 5, 6 - topi, (nw_lon, n_lat))
    to_s = copy(send_r.at[1], recv_r.at[0], 3, 2, (lon, s_lat))
    to_se = copy(pack.at[pl.ds(0, 8)], ext.at[1, up], 6, 5, (e_lon, s_lat))
    to_sw = copy(pack.at[pl.ds(0, 8)], ext.at[0, up], 7, 4, (w_lon, s_lat))
    from_s = copy(send_r.at[0], recv_r.at[1], 2, 3, (lon, s_lat))
    from_se = copy(corner, ext.at[0, down], 5, 6, (e_lon, s_lat))
    from_sw = copy(corner, ext.at[1, down], 4, 7, (w_lon, s_lat))

    to_east.start()
    to_west.start()

    @pl.when(ne_other)
    def _():
        to_ne.start()

    @pl.when(nw_other)
    def _():
        to_nw.start()

    @pl.when(inner)
    def _():
        to_se.start()
        to_sw.start()

    def take_edges(c, at):
        return st[at, pl.ds(PAD, 2), :], st[at, pl.ds(PAD + rows - 2, 2), :]

    def put_edges(c, at, low, high):
        send_r[1, pl.ds(2 * c, 2), :] = low
        send_r[0, pl.ds(2 * c, 2), :] = high
        st[at, pl.ds(row0, 2), :] = high
        st[at, pl.ds(row0 + 6, 2), :] = low

    entries(take_edges, put_edges)

    @pl.when(top)
    def _():
        tiles = [send_r[0, pl.ds(8 * t, 8), :] for t in range(2 * ENTRIES // 8)]
        tiles = [jnp.where((sub & 1) == 1, pltpu.roll(v, 1, 0), pltpu.roll(v, 7, 0)) for v in tiles]
        step = 1
        while step < cols:
            far_half = (lane & step) != 0
            tiles = [jnp.where(far_half, pltpu.roll(v, step, 1), pltpu.roll(v, cols - step, 1)) for v in tiles]
            step *= 2
        for t, v in enumerate(tiles):
            send_r[0, pl.ds(8 * t, 8), :] = -v if 4 * LEVELS <= 8 * t < 8 * LEVELS else v

    to_n.start()

    @pl.when(inner)
    def _():
        to_s.start()

    is_east = (lane & 3) == 2

    def arrive():
        to_s.wait_recv()

        @pl.when(inner)
        def _():
            from_s.wait_recv()
            from_se.wait_recv()
            from_sw.wait_recv()

        @pl.when(ne_other)
        def _():
            to_sw.wait_recv()

        @pl.when(nw_other)
        def _():
            to_se.wait_recv()

        to_west.wait_recv()
        to_east.wait_recv()

        pair = (lax.broadcasted_iota(jnp.int32, (128, 128), 1) >> 1) & 1

        own = pack[...]
        about = [jnp.transpose(jnp.where(pair != side, ext[side], own)) for side in range(2)]
        for side in range(2):
            z[side] = about[side]

        def take_halo(c, at):
            two, four = pl.ds(2 * c, 2), pl.ds(4 * c, 4)
            return recv_r[0, two, :], recv_r[1, two, :], z[0, four, :], z[1, four, :]

        def put_halo(c, at, north, south, east, west):
            st[at, pl.ds(PAD + rows, 1), :] = north[0:1, :]
            st[at, pl.ds(PAD - 1, 1), :] = south[1:2, :]
            st[at, pl.ds(row0 + 2, 2), :] = north
            st[at, pl.ds(row0 + 4, 2), :] = south
            st[at, pl.ds(col0, 4), :] = east
            st[at, pl.ds(col0 + 4, 4), :] = west

        entries(take_halo, put_halo)
        st[met0 + 3, pl.ds(col0, 8), :] = -st[met0 + 3, pl.ds(col0, 8), :]

        @pl.loop(0, chunks)
        def _(r):
            span = pl.ds(pl.multiple_of(8 * r, 8), 8)
            hold[0, pl.ds(pl.multiple_of(PAD + 8 * r, 8), 8), :] = jnp.where(is_east, ext[0, span, :], ext[1, span, :])

        far_n = jnp.where(is_east, ext[0, up, :], ext[1, up, :])[0:1, :]
        far_s = jnp.where(is_east, ext[0, down, :], ext[1, down, :])[7:8, :]
        hold[0, pl.ds(row0, 8), :] = jnp.where(
            sub == 2, jnp.broadcast_to(far_n, (8, 128)), jnp.broadcast_to(far_s, (8, 128))
        )

    def between():
        @pl.loop(0, 5 * LEVELS // 4)
        def _(g):
            held = [(st[FIELDS + 4 * g + i, pl.ds(row0, 8), :], st[FIELDS + 4 * g + i, pl.ds(col0, 8), :]) for i in range(4)]
            for i, (about_row, about_col) in enumerate(held):
                c = 4 * g + i
                st[FIELDS + c, pl.ds(PAD + rows, 1), :] = about_row[2:3, :]
                st[FIELDS + c, pl.ds(PAD - 1, 1), :] = about_row[5:6, :]
                z[0, pl.ds(4 * c + 2, 1), :] = about_col[2:3, :]
                z[0, pl.ds(4 * c + 1, 1), :] = about_col[5:6, :]
                z[1, pl.ds(4 * c + 2, 1), :] = about_col[6:7, :]
                z[1, pl.ds(4 * c + 1, 1), :] = about_col[1:2, :]

        hold[1, body, :] = jnp.transpose(z[0])[:rows, :]
        hold[0, body, :] = jnp.transpose(z[1])[:rows, :]

        @pl.loop(0, (chunks - 2) // 2)
        def _(r):
            outer = jnp.logical_or(lane == 0, lane == 127)
            patched = []
            for i in range(2):
                held = pl.ds(pl.multiple_of(PAD + 8 * (1 + 2 * r + i), 8), 8)
                own = hold[0, held, :]
                for c in range(FIELDS):
                    ends = pltpu.roll(own, (126 - 4 * placed(c)) % 128, 1)
                    patched.append((c, held, jnp.where(outer, ends, st[FIELDS + c, held, :])))
            for c, held, val in patched:
                st[FIELDS + c, held, :] = val

    ahead = (chunks - 2) // 2
    flag = lambda cond: cond.astype(jnp.int32)

    def tile_values(p, i):
        second = flag(p >= ahead + 2)
        early = flag(p < ahead)
        outer = flag(p == ahead)
        slabs = flag(p == ahead + 1)
        tile = (
            early * (1 + 2 * p + i) + outer * (i * (chunks - 1)) + slabs * (chunks + i)
            + second * (2 * (p - ahead - 2) + i)
        )
        off = pl.multiple_of(PAD + 8 * (tile + slabs), 8)
        held = pl.ds(off, 8)
        src = FIELDS * second
        dst = FIELDS - src
        turned_tile = early + slabs * i
        at_first = lane == 0 - turned_tile
        at_last = lane == 127 + turned_tile
        ends_all = hold[second, held, :]

        def side_of(c, val):
            ends = pltpu.roll(ends_all, (126 - 4 * placed(c)) % 128, 1)
            east = pltpu.roll(jnp.where(at_first, ends, val), 127, 1)
            west = pltpu.roll(jnp.where(at_last, ends, val), 1, 1)
            return east, west

        def around(c, at):
            val = st[at, held, :]
            return (val, *side_of(c, val), st[at, pl.ds(off + 1, 8), :], st[at, pl.ds(off - 1, 8), :])

        floor, zs, ms, rot, eddy, *mix = [st[met0 + m, held, :] for m in range(8)]
        rz, rm = 1.0 / zs, 1.0 / ms
        kx, ky, hx, hy = eddy * rz * rz, eddy * rm * rm, 0.5 * rz, 0.5 * rm
        results = []
        sum_x = sum_y = None
        for k in range(LEVELS):
            wet, we, ww, wn, ws = around(WET * LEVELS + k, wet0 + k)
            dtw = TIME_STEP * wet
            ax, ay = dtw * kx, dtw * ky
            bx, by, br = dtw * hx, dtw * hy, dtw * rot
            ae, aw, an, as_ = ax * we, ax * ww, ay * wn, ay * ws
            centre = 1.0 - (ae + aw) - (an + as_)
            t2 = dtw * inv_h2[k]
            below = above = None
            if k < LEVELS - 1:
                below = t2 * mix[k] * st[wet0 + k + 1, held, :]
                centre = centre - below
            if k > 0:
                above = t2 * mix[k - 1] * st[wet0 + k - 1, held, :]
                centre = centre - above
            drag = centre - jnp.where(floor == float(k), BOTTOM_DRAG * dtw, 0.0)
            u, v = st[src + 2 * LEVELS + k, held, :], st[src + 3 * LEVELS + k, held, :]
            bu, bv = bx * u, by * v
            ce, cw, cn, cs = ae - bu, aw + bu, an - bv, as_ + bv
            layer_x = layer_y = None
            for ch in range(4):
                c = ch * LEVELS + k
                val, east, west, north, south = around(c, src + c)
                new = (centre if ch < 2 else drag) * val + (ce * east + cw * west) + (cn * north + cs * south)
                if below is not None:
                    new = new + below * st[src + c + 1, held, :]
                if above is not None:
                    new = new + above * st[src + c - 1, held, :]
                if ch == 0:
                    layer_x, layer_y = EXPANSION * (west - east), EXPANSION * (south - north)
                if ch == 1:
                    layer_x = (layer_x + CONTRACTION * (east - west)) * heights[k]
                    layer_y = (layer_y + CONTRACTION * (north - south)) * heights[k]
                    sum_x = layer_x if k == 0 else sum_x + layer_x
                    sum_y = layer_y if k == 0 else sum_y + layer_y
                if ch == 2:
                    new = new + br * v - bx * (sum_x - 0.5 * layer_x)
                if ch == 3:
                    new = new - br * u - by * (sum_y - 0.5 * layer_y)
                results.append((c, new))
        return dst, held, results

    @pl.loop(0, ahead + 2 + chunks // 2)
    def _(p):
        pl.when(p == ahead)(arrive)
        pl.when(p == ahead + 2)(between)
        done = [tile_values(p, i) for i in range(2)]
        for dst, held, results in done:
            for c, new in results:
                st[dst + c, held, :] = new

    @pl.loop(0, chunks // 2)
    def _(r):
        held = pl.ds(pl.multiple_of(PAD + 16 * r, 8), 16)
        vals = [st[c, held, :] for c in range(FIELDS)]
        for c in range(FIELDS):
            outs[c // LEVELS][c % LEVELS, pl.ds(pl.multiple_of(16 * r, 16), 16), :] = vals[c]

    to_east.wait_send()
    to_west.wait_send()
    to_n.wait_send()

    @pl.when(ne_other)
    def _():
        to_ne.wait_send()

    @pl.when(nw_other)
    def _():
        to_nw.wait_send()

    @pl.when(inner)
    def _():
        to_s.wait_send()
        to_se.wait_send()
        to_sw.wait_send()


def hand_over(*refs):
    moves = [pltpu.make_async_copy(refs[c], refs[4 + c], refs[8].at[c]) for c in range(4)]
    for move in moves:
        move.start()
    for move in moves:
        move.wait()


def solution(mesh):
    nlon, nlat = mesh.shape["lon"], mesh.shape["lat"]

    def shards(*args):
        levels, rows, cols = args[0].shape
        f32 = jnp.float32
        vmem = pltpu.VMEM
        held = rows + 5 * PAD
        hbm = pl.BlockSpec(memory_space=pltpu.HBM)
        out_shape = [jax.ShapeDtypeStruct((levels, rows, cols), f32)] * 4
        results = pl.pallas_call(
            functools.partial(kernel, nlon, nlat, rows, cols),
            out_shape=[pltpu.VMEM((levels, rows, cols), f32)] * 4,
            in_specs=[hbm] * 11 + [pl.BlockSpec(memory_space=pltpu.SMEM)],
            out_specs=[pl.BlockSpec(memory_space=pltpu.VMEM)] * 4,
            scratch_shapes=[
                vmem((2 * FIELDS + ENTRIES - FIELDS, held, cols), f32),
                vmem((2, held, 128), f32),
                vmem((levels, rows, cols), jnp.int32),
                vmem((rows, cols), jnp.int32),
                vmem((128, 128), f32),
                vmem((2, 128, 128), f32),
                vmem((2, 2 * ENTRIES, cols), f32),
                vmem((2, 2 * ENTRIES, cols), f32),
                vmem((8, 128), f32),
                vmem((2, 128, 128), f32),
                pltpu.SemaphoreType.DMA((11,)),
                pltpu.SemaphoreType.DMA((8,)),
                pltpu.SemaphoreType.DMA((8,)),
            ],
            compiler_params=pltpu.CompilerParams(
                collective_id=0, has_side_effects=True, vmem_limit_bytes=60 * 1024 * 1024
            ),
        )(*args)
        return tuple(pl.pallas_call(
            hand_over,
            out_shape=out_shape,
            in_specs=[pl.BlockSpec(memory_space=pltpu.VMEM)] * 4,
            out_specs=[hbm] * 4,
            scratch_shapes=[pltpu.SemaphoreType.DMA((4,))],
            compiler_params=pltpu.CompilerParams(vmem_limit_bytes=16 * 1024 * 1024),
        )(*results))

    field, plane = P(None, "lat", "lon"), P("lat", "lon")
    return jax.shard_map(
        shards,
        mesh=mesh,
        in_specs=(field,) * 5 + (plane,) * 5 + (field, P()),
        out_specs=(field,) * 4,
        check_vma=False,
    )
```

```python
import functools

import jax
import jax.numpy as jnp
from jax import lax
from jax.experimental import pallas as pl
from jax.experimental.pallas import tpu as pltpu
from jax.sharding import PartitionSpec as P

MESH = pl.DeviceIdType.MESH
TIME_STEP = 0.25
EXPANSION = 0.2
CONTRACTION = 0.8
BOTTOM_DRAG = 1.0
LEVELS = 4
ENTRIES = 28
FIELDS = 16
WET = 4
PAD = 8


def placed(c):
    if 8 <= c < 12:
        return c + 4
    if 12 <= c < 16:
        return c - 4
    return {21: 22, 22: 21}.get(c, c)


def kernel(nlon, nlat, rows, cols, *refs):
    ins, h_ref = refs[:11], refs[11]
    outs = refs[12:16]
    (st, hold, wet_i, floor_i, pack, ext, send_r, recv_r, corner, z, in_sem, s_sem, r_sem) = refs[16:]
    lon, lat = lax.axis_index("lon"), lax.axis_index("lat")
    top, bottom = lat == nlat - 1, lat == 0
    topi = top.astype(jnp.int32)
    f32 = jnp.float32
    chunks = rows // 8
    row_tile, col_tile = chunks, chunks + 1
    row0, col0 = PAD + 8 * (chunks + 1), PAD + 8 * (chunks + 2)
    body = pl.ds(PAD, rows)

    wet0, met0 = 2 * FIELDS, 2 * FIELDS + LEVELS
    loads = [pltpu.make_async_copy(ins[c], st.at[pl.ds(4 * c, 4), body], in_sem.at[c]) for c in range(4)]
    loads.append(pltpu.make_async_copy(ins[4], wet_i, in_sem.at[4]))
    loads.append(pltpu.make_async_copy(ins[5], floor_i, in_sem.at[5]))
    loads += [pltpu.make_async_copy(ins[6 + m], st.at[met0 + 1 + m, body], in_sem.at[6 + m]) for m in range(4)]
    loads.append(pltpu.make_async_copy(ins[10], st.at[pl.ds(met0 + 5, 3), body], in_sem.at[10]))
    for load in loads:
        load.start()

    e_lon, w_lon = lax.rem(lon + 1, nlon), lax.rem(lon + nlon - 1, nlon)
    n_lat = jnp.where(top, lat, lat + 1)
    n_lon = jnp.where(top, nlon - 1 - lon, lon)
    ne_lon = jnp.where(top, lax.rem(2 * nlon - 2 - lon, nlon), e_lon)
    nw_lon = jnp.where(top, lax.rem(nlon - lon, nlon), w_lon)
    s_lat = jnp.maximum(lat - 1, 0)
    ne_self = jnp.logical_and(top, ne_lon == lon)
    nw_self = jnp.logical_and(top, nw_lon == lon)
    ne_other = jnp.logical_not(ne_self)
    nw_other = jnp.logical_not(nw_self)
    inner = jnp.logical_not(bottom)

    @pl.when(bottom)
    def _():
        ext[0, 120:, :] = jnp.zeros((8, 128), f32)
        ext[1, 120:, :] = jnp.zeros((8, 128), f32)
        recv_r[1, : 2 * 5 * LEVELS, :] = jnp.zeros((2 * 5 * LEVELS, cols), f32)
        recv_r[1, 2 * 5 * LEVELS :, :] = jnp.ones((2 * ENTRIES - 10 * LEVELS, cols), f32)

    barrier = pltpu.get_barrier_semaphore()

    def greet(dev):
        pl.semaphore_signal(barrier, inc=1, device_id=dev, device_id_type=MESH)

    greet((e_lon, lat))
    greet((w_lon, lat))
    greet((n_lon, n_lat))

    @pl.when(ne_other)
    def _():
        greet((ne_lon, n_lat))

    @pl.when(nw_other)
    def _():
        greet((nw_lon, n_lat))

    @pl.when(inner)
    def _():
        greet((lon, s_lat))
        greet((e_lon, s_lat))
        greet((w_lon, s_lat))

    lane = lax.broadcasted_iota(jnp.int32, (8, 128), 1)
    sub = lax.broadcasted_iota(jnp.int32, (8, 128), 0)
    heights = [jnp.full((8, 128), h_ref[k], f32) for k in range(LEVELS)]
    inv_h2 = [1.0 / (h * h) for h in heights]

    for load in loads:
        load.wait()

    group = lane >> 2

    def masked(r):
        span = pl.ds(pl.multiple_of(8 * r, 8), 8)
        held = pl.ds(pl.multiple_of(PAD + 8 * r, 8), 8)
        packed = jnp.zeros((8, 128), f32)
        kept = []
        wet = [wet_i[k, span, :].astype(f32) for k in range(LEVELS)]
        for c in range(ENTRIES):
            ch, k = c // LEVELS, c % LEVELS
            at = c if ch < WET else c + FIELDS
            if ch < WET:
                val = st[at, held, :] * wet[k]
            elif ch == WET:
                val = wet[k]
            elif at == met0:
                val = floor_i[span, :].astype(f32)
            else:
                val = st[at, held, :]
            if at <= met0:
                kept.append((at, val))
            g = placed(c)
            packed = jnp.where(group == g, pltpu.roll(val, (4 * g + 2) % 128, 1), packed)
        return span, held, packed, kept

    @pl.loop(0, chunks // 2)
    def _(r):
        for span, held, packed, kept in [masked(2 * r + i) for i in range(2)]:
            pack[span, :] = packed
            for at, val in kept:
                st[at, held, :] = val

    def entries(load, save):
        for g in range(ENTRIES // 4):
            at = 4 * g + (FIELDS if g >= FIELDS // 4 else 0)
            held = [load(4 * g + i, at + i) for i in range(4)]
            for i in range(4):
                save(4 * g + i, at + i, *held[i])

    last = pack[pl.ds(rows - 8, 8), :]
    turned = jnp.broadcast_to(last[7:8, :], (8, 128))
    for step in (1, 2):
        turned = jnp.where((lane & step) != 0, pltpu.roll(turned, step, 1), pltpu.roll(turned, 128 - step, 1))
    turned = jnp.where(jnp.logical_and(lane >= 8 * LEVELS, lane < 16 * LEVELS), -turned, turned)
    top_v = jnp.full((8, 128), topi) == 1
    folded = jnp.where(top_v, turned, last)
    corner[...] = folded

    @pl.when(ne_self)
    def _():
        ext[0, pl.ds(rows, 8), :] = folded

    @pl.when(nw_self)
    def _():
        ext[1, pl.ds(rows, 8), :] = folded

    pl.semaphore_wait(
        barrier,
        3 + ne_other.astype(jnp.int32) + nw_other.astype(jnp.int32) + 3 * inner.astype(jnp.int32),
    )

    def copy(src, dst, s, r, dev):
        return pltpu.make_async_remote_copy(
            src_ref=src, dst_ref=dst, send_sem=s_sem.at[s], recv_sem=r_sem.at[r], device_id=dev, device_id_type=MESH
        )

    whole, up, down = pl.ds(0, rows), pl.ds(rows, 8), pl.ds(120, 8)
    over = pl.ds(pl.multiple_of(120 - (120 - rows) * topi, 8), 8)
    to_east = copy(pack.at[whole], ext.at[1, whole], 0, 1, (e_lon, lat))
    to_west = copy(pack.at[whole], ext.at[0, whole], 1, 0, (w_lon, lat))
    to_n = copy(send_r.at[0], recv_r.at[1 - topi], 2, 3 - topi, (n_lon, n_lat))
    to_ne = copy(corner, ext.at[1 - topi, over], 4, 7 - 3 * topi, (ne_lon, n_lat))
    to_nw = copy(corner, ext.at[topi, over], 5, 6 - topi, (nw_lon, n_lat))
    to_s = copy(send_r.at[1], recv_r.at[0], 3, 2, (lon, s_lat))
    to_se = copy(pack.at[pl.ds(0, 8)], ext.at[1, up], 6, 5, (e_lon, s_lat))
    to_sw = copy(pack.at[pl.ds(0, 8)], ext.at[0, up], 7, 4, (w_lon, s_lat))
    from_s = copy(send_r.at[0], recv_r.at[1], 2, 3, (lon, s_lat))
    from_se = copy(corner, ext.at[0, down], 5, 6, (e_lon, s_lat))
    from_sw = copy(corner, ext.at[1, down], 4, 7, (w_lon, s_lat))

    to_east.start()
    to_west.start()

    @pl.when(ne_other)
    def _():
        to_ne.start()

    @pl.when(nw_other)
    def _():
        to_nw.start()

    @pl.when(inner)
    def _():
        to_se.start()
        to_sw.start()

    def take_edges(c, at):
        return st[at, pl.ds(PAD, 2), :], st[at, pl.ds(PAD + rows - 2, 2), :]

    def put_edges(c, at, low, high):
        send_r[1, pl.ds(2 * c, 2), :] = low
        send_r[0, pl.ds(2 * c, 2), :] = high
        st[at, pl.ds(row0, 2), :] = high
        st[at, pl.ds(row0 + 6, 2), :] = low

    entries(take_edges, put_edges)

    @pl.when(top)
    def _():
        tiles = [send_r[0, pl.ds(8 * t, 8), :] for t in range(2 * ENTRIES // 8)]
        tiles = [jnp.where((sub & 1) == 1, pltpu.roll(v, 1, 0), pltpu.roll(v, 7, 0)) for v in tiles]
        step = 1
        while step < cols:
            far_half = (lane & step) != 0
            tiles = [jnp.where(far_half, pltpu.roll(v, step, 1), pltpu.roll(v, cols - step, 1)) for v in tiles]
            step *= 2
        for t, v in enumerate(tiles):
            send_r[0, pl.ds(8 * t, 8), :] = -v if 4 * LEVELS <= 8 * t < 8 * LEVELS else v

    to_n.start()

    @pl.when(inner)
    def _():
        to_s.start()

    is_east = (lane & 3) == 2

    def arrive():
        to_s.wait_recv()

        @pl.when(inner)
        def _():
            from_s.wait_recv()
            from_se.wait_recv()
            from_sw.wait_recv()

        @pl.when(ne_other)
        def _():
            to_sw.wait_recv()

        @pl.when(nw_other)
        def _():
            to_se.wait_recv()

        to_west.wait_recv()
        to_east.wait_recv()

        pair = (lax.broadcasted_iota(jnp.int32, (128, 128), 1) >> 1) & 1

        own = pack[...]
        about = [jnp.transpose(jnp.where(pair != side, ext[side], own)) for side in range(2)]
        for side in range(2):
            z[side] = about[side]

        def take_halo(c, at):
            two, four = pl.ds(2 * c, 2), pl.ds(4 * c, 4)
            return recv_r[0, two, :], recv_r[1, two, :], z[0, four, :], z[1, four, :]

        def put_halo(c, at, north, south, east, west):
            st[at, pl.ds(PAD + rows, 1), :] = north[0:1, :]
            st[at, pl.ds(PAD - 1, 1), :] = south[1:2, :]
            st[at, pl.ds(row0 + 2, 2), :] = north
            st[at, pl.ds(row0 + 4, 2), :] = south
            st[at, pl.ds(col0, 4), :] = east
            st[at, pl.ds(col0 + 4, 4), :] = west

        entries(take_halo, put_halo)
        st[met0 + 3, pl.ds(col0, 8), :] = -st[met0 + 3, pl.ds(col0, 8), :]

        @pl.loop(0, chunks)
        def _(r):
            span = pl.ds(pl.multiple_of(8 * r, 8), 8)
            hold[0, pl.ds(pl.multiple_of(PAD + 8 * r, 8), 8), :] = jnp.where(is_east, ext[0, span, :], ext[1, span, :])

        far_n = jnp.where(is_east, ext[0, up, :], ext[1, up, :])[0:1, :]
        far_s = jnp.where(is_east, ext[0, down, :], ext[1, down, :])[7:8, :]
        hold[0, pl.ds(row0, 8), :] = jnp.where(
            sub == 2, jnp.broadcast_to(far_n, (8, 128)), jnp.broadcast_to(far_s, (8, 128))
        )

    def between():
        for g in range(5 * LEVELS // 4):
            held = [(st[FIELDS + 4 * g + i, pl.ds(row0, 8), :], st[FIELDS + 4 * g + i, pl.ds(col0, 8), :]) for i in range(4)]
            for i, (about_row, about_col) in enumerate(held):
                c = 4 * g + i
                st[FIELDS + c, pl.ds(PAD + rows, 1), :] = about_row[2:3, :]
                st[FIELDS + c, pl.ds(PAD - 1, 1), :] = about_row[5:6, :]
                z[0, pl.ds(4 * c + 2, 1), :] = about_col[2:3, :]
                z[0, pl.ds(4 * c + 1, 1), :] = about_col[5:6, :]
                z[1, pl.ds(4 * c + 2, 1), :] = about_col[6:7, :]
                z[1, pl.ds(4 * c + 1, 1), :] = about_col[1:2, :]

        hold[1, body, :] = jnp.transpose(z[0])[:rows, :]
        hold[0, body, :] = jnp.transpose(z[1])[:rows, :]

        @pl.loop(0, (chunks - 2) // 2)
        def _(r):
            outer = jnp.logical_or(lane == 0, lane == 127)
            patched = []
            for i in range(2):
                held = pl.ds(pl.multiple_of(PAD + 8 * (1 + 2 * r + i), 8), 8)
                own = hold[0, held, :]
                for c in range(FIELDS):
                    ends = pltpu.roll(own, (126 - 4 * placed(c)) % 128, 1)
                    patched.append((c, held, jnp.where(outer, ends, st[FIELDS + c, held, :])))
            for c, held, val in patched:
                st[FIELDS + c, held, :] = val

    ahead = (chunks - 2) // 2
    flag = lambda cond: cond.astype(jnp.int32)

    def tile_values(p, i):
        second = flag(p >= ahead + 2)
        early = flag(p < ahead)
        outer = flag(p == ahead)
        slabs = flag(p == ahead + 1)
        tile = (
            early * (1 + 2 * p + i) + outer * (i * (chunks - 1)) + slabs * (chunks + i)
            + second * (2 * (p - ahead - 2) + i)
        )
        off = pl.multiple_of(PAD + 8 * (tile + slabs), 8)
        held = pl.ds(off, 8)
        src = FIELDS * second
        dst = FIELDS - src
        turned_tile = early + slabs * i
        at_first = lane == 0 - turned_tile
        at_last = lane == 127 + turned_tile
        ends_all = hold[second, held, :]

        def side_of(c, val):
            ends = pltpu.roll(ends_all, (126 - 4 * placed(c)) % 128, 1)
            east = pltpu.roll(jnp.where(at_first, ends, val), 127, 1)
            west = pltpu.roll(jnp.where(at_last, ends, val), 1, 1)
            return east, west

        def around(c, at):
            val = st[at, held, :]
            return (val, *side_of(c, val), st[at, pl.ds(off + 1, 8), :], st[at, pl.ds(off - 1, 8), :])

        floor, zs, ms, rot, eddy, *mix = [st[met0 + m, held, :] for m in range(8)]
        rz, rm = 1.0 / zs, 1.0 / ms
        kx, ky, hx, hy = eddy * rz * rz, eddy * rm * rm, 0.5 * rz, 0.5 * rm
        results = []
        sum_x = sum_y = None
        for k in range(LEVELS):
            wet, we, ww, wn, ws = around(WET * LEVELS + k, wet0 + k)
            dtw = TIME_STEP * wet
            ax, ay = dtw * kx, dtw * ky
            bx, by, br = dtw * hx, dtw * hy, dtw * rot
            ae, aw, an, as_ = ax * we, ax * ww, ay * wn, ay * ws
            centre = 1.0 - (ae + aw) - (an + as_)
            t2 = dtw * inv_h2[k]
            below = above = None
            if k < LEVELS - 1:
                below = t2 * mix[k] * st[wet0 + k + 1, held, :]
                centre = centre - below
            if k > 0:
                above = t2 * mix[k - 1] * st[wet0 + k - 1, held, :]
                centre = centre - above
            drag = centre - jnp.where(floor == float(k), BOTTOM_DRAG * dtw, 0.0)
            u, v = st[src + 2 * LEVELS + k, held, :], st[src + 3 * LEVELS + k, held, :]
            bu, bv = bx * u, by * v
            ce, cw, cn, cs = ae - bu, aw + bu, an - bv, as_ + bv
            layer_x = layer_y = None
            for ch in range(4):
                c = ch * LEVELS + k
                val, east, west, north, south = around(c, src + c)
                new = (centre if ch < 2 else drag) * val + (ce * east + cw * west) + (cn * north + cs * south)
                if below is not None:
                    new = new + below * st[src + c + 1, held, :]
                if above is not None:
                    new = new + above * st[src + c - 1, held, :]
                if ch == 0:
                    layer_x, layer_y = EXPANSION * (west - east), EXPANSION * (south - north)
                if ch == 1:
                    layer_x = (layer_x + CONTRACTION * (east - west)) * heights[k]
                    layer_y = (layer_y + CONTRACTION * (north - south)) * heights[k]
                    sum_x = layer_x if k == 0 else sum_x + layer_x
                    sum_y = layer_y if k == 0 else sum_y + layer_y
                if ch == 2:
                    new = new + br * v - bx * (sum_x - 0.5 * layer_x)
                if ch == 3:
                    new = new - br * u - by * (sum_y - 0.5 * layer_y)
                results.append((c, new))
        return dst, held, results

    @pl.loop(0, ahead + 2 + chunks // 2)
    def _(p):
        pl.when(p == ahead)(arrive)
        pl.when(p == ahead + 2)(between)
        done = [tile_values(p, i) for i in range(2)]
        for dst, held, results in done:
            for c, new in results:
                st[dst + c, held, :] = new

    @pl.loop(0, chunks // 2)
    def _(r):
        held = pl.ds(pl.multiple_of(PAD + 16 * r, 8), 16)
        vals = [st[c, held, :] for c in range(FIELDS)]
        for c in range(FIELDS):
            outs[c // LEVELS][c % LEVELS, pl.ds(pl.multiple_of(16 * r, 16), 16), :] = vals[c]

    to_east.wait_send()
    to_west.wait_send()
    to_n.wait_send()

    @pl.when(ne_other)
    def _():
        to_ne.wait_send()

    @pl.when(nw_other)
    def _():
        to_nw.wait_send()

    @pl.when(inner)
    def _():
        to_s.wait_send()
        to_se.wait_send()
        to_sw.wait_send()


def hand_over(*refs):
    moves = [pltpu.make_async_copy(refs[c], refs[4 + c], refs[8].at[c]) for c in range(4)]
    for move in moves:
        move.start()
    for move in moves:
        move.wait()


def solution(mesh):
    nlon, nlat = mesh.shape["lon"], mesh.shape["lat"]

    def shards(*args):
        levels, rows, cols = args[0].shape
        f32 = jnp.float32
        vmem = pltpu.VMEM
        held = rows + 5 * PAD
        hbm = pl.BlockSpec(memory_space=pltpu.HBM)
        out_shape = [jax.ShapeDtypeStruct((levels, rows, cols), f32)] * 4
        results = pl.pallas_call(
            functools.partial(kernel, nlon, nlat, rows, cols),
            out_shape=[pltpu.VMEM((levels, rows, cols), f32)] * 4,
            in_specs=[hbm] * 11 + [pl.BlockSpec(memory_space=pltpu.SMEM)],
            out_specs=[pl.BlockSpec(memory_space=pltpu.VMEM)] * 4,
            scratch_shapes=[
                vmem((2 * FIELDS + ENTRIES - FIELDS, held, cols), f32),
                vmem((2, held, 128), f32),
                vmem((levels, rows, cols), jnp.int32),
                vmem((rows, cols), jnp.int32),
                vmem((128, 128), f32),
                vmem((2, 128, 128), f32),
                vmem((2, 2 * ENTRIES, cols), f32),
                vmem((2, 2 * ENTRIES, cols), f32),
                vmem((8, 128), f32),
                vmem((2, 128, 128), f32),
                pltpu.SemaphoreType.DMA((11,)),
                pltpu.SemaphoreType.DMA((8,)),
                pltpu.SemaphoreType.DMA((8,)),
            ],
            compiler_params=pltpu.CompilerParams(
                collective_id=0, has_side_effects=True, vmem_limit_bytes=60 * 1024 * 1024
            ),
        )(*args)
        return tuple(pl.pallas_call(
            hand_over,
            out_shape=out_shape,
            in_specs=[pl.BlockSpec(memory_space=pltpu.VMEM)] * 4,
            out_specs=[hbm] * 4,
            scratch_shapes=[pltpu.SemaphoreType.DMA((4,))],
            compiler_params=pltpu.CompilerParams(vmem_limit_bytes=16 * 1024 * 1024),
        )(*results))

    field, plane = P(None, "lat", "lon"), P("lat", "lon")
    return jax.shard_map(
        shards,
        mesh=mesh,
        in_specs=(field,) * 5 + (plane,) * 5 + (field, P()),
        out_specs=(field,) * 4,
        check_vma=False,
    )
```
